32 devices in a mesh: section: 2 (over x), dp: 4 (over z), tensor: 4 (over y, core).
Axes of the slice: x: 2, y: 2, z: 4, core: 2. Of those that a mesh axis runs over, the one named last changes fastest.
Arguments:
- boundary: bfloat16 [2, 8, 1024, 1024], P('section', 'dp', 'tensor'), may hold values from -6 to 6
- conditioning: bfloat16 [8, 1024], P('dp'), may hold values from -6 to 6
- query_key_value_weight: bfloat16 [2, 1024, 3, 1024], P('section', None, None, 'tensor'), may hold values from -0.1875 to 0.1875
- query_value_bias: bfloat16 [2, 2, 1024], P('section', None, 'tensor'), may hold values from -3 to 3
- attention_output_weight: bfloat16 [2, 1024, 1024], P('section', None, 'tensor'), may hold values from -1.5 to 1.5
- output_biases: bfloat16 [2, 2, 1024], P('section'), may hold values from -3 to 3
- first_mlp_weight: bfloat16 [2, 1024, 4096], P('section', None, 'tensor'), may hold values from -0.1875 to 0.1875
- first_mlp_bias: bfloat16 [2, 4096], P('section', 'tensor'), may hold values from -3 to 3
- second_mlp_weight: bfloat16 [2, 1024, 4096], P('section', None, 'tensor'), may hold values from -0.09375 to 0.09375
- w_ada: bfloat16 [2, 1024, 6144], P('section'), may hold values from -0.1875 to 0.1875
- ada_bias: bfloat16 [2, 6144], P('section'), may hold values from -3 to 3
Outputs:
- boundary_out: bfloat16 [2, 8, 1024, 1024], P('section', 'dp', 'tensor')
- cond_grad: float32 [8, 1024], P('dp')
- grad_qkv: float32 [2, 1024, 3, 1024], P('section', 'dp', None, 'tensor')
- grad_qv_bias: float32 [2, 2048], P('section', ('dp', 'tensor'))
- grad_proj: float32 [2, 1024, 1024], P('section', 'dp', 'tensor')
- grad_out_bias: float32 [2, 2048], P('section', ('dp', 'tensor'))
- grad_fc1: float32 [2, 1024, 4096], P('section', 'dp', 'tensor')
- grad_fc1_bias: float32 [2, 4096], P('section', ('dp', 'tensor'))
- grad_fc2: float32 [2, 1024, 4096], P('section', 'dp', 'tensor')
- grad_ada: float32 [2, 1024, 6144], P('section', ('dp', 'tensor'))
- grad_ada_bias: float32 [2, 6144], P('section', ('dp', 'tensor'))
The draws below stay inside these ranges and needn't reach their ends.
All inputs are finite; a program needn't handle non-finite values.
Results may differ from the reference program's by a relative error of at most 0.015.
Values may be sent and summed in bfloat16 or wider, within the bound.
No kernel may reach another device: no remote copies, remote signals or barrier semaphores. Data moves between devices by JAX's collectives and lax.ppermute only.
A program may use at most 256 MiB of HBM per device.

```python
import jax
import jax.numpy as jnp
from jax import lax

D = 1024
HEADS = 16
HD = 64
FF = 4096
SEQ = 1024
LAYERS = 2
LATENTS = 8


def shard_levels(stream_key, dims, split, least, high):
    def one(dim, parts):
        draws = jax.random.uniform(jax.random.fold_in(jax.random.fold_in(stream_key, 6), dim), (parts,), jnp.float32, least / len(split), high / len(split))
        return jnp.repeat(jnp.exp(draws), dims[dim] // parts).reshape((-1,) + (1,) * (len(dims) - dim - 1))

    factor_of = one(*split[0])
    for cut in split[1:]:
        factor_of = factor_of * one(*cut)
    return factor_of


def scatter_about(own_key, dims, scale, most, split=(), kind=jnp.bfloat16):
    values = scale * jax.random.normal(own_key, dims, jnp.float32)
    if split:
        values = values * shard_levels(own_key, dims, split, -0.22, 0.18)
    return jnp.clip(values, -most, most).astype(kind)


def setup_inputs(seed: int = 0) -> dict:
    key_of = jax.random.split(jax.random.key(seed), 12)
    return {
        "boundary": scatter_about(key_of[0], (2, LATENTS, SEQ, D), 1.0, 6.0, ((0, 2), (1, 4), (2, 4))),
        "conditioning": scatter_about(key_of[1], (LATENTS, D), 1.0, 6.0, ((0, 4),)),
        "query_key_value_weight": scatter_about(key_of[2], (LAYERS, D, 3, D), D ** -0.5, 0.1875, ((0, 2), (3, 4))),
        "query_value_bias": scatter_about(key_of[3], (LAYERS, 2, D), 0.5, 3.0, ((0, 2), (2, 4))),
        "attention_output_weight": scatter_about(key_of[4], (LAYERS, D, D), (D * 16 // SEQ) ** -0.5, 1.5, ((0, 2), (2, 4))),
        "output_biases": scatter_about(key_of[5], (LAYERS, 2, D), 0.5, 3.0, ((0, 2),)),
        "first_mlp_weight": scatter_about(key_of[6], (LAYERS, D, FF), D ** -0.5, 0.1875, ((0, 2), (2, 4))),
        "first_mlp_bias": scatter_about(key_of[7], (LAYERS, FF), 0.5, 3.0, ((0, 2), (1, 4))),
        "second_mlp_weight": scatter_about(key_of[8], (LAYERS, D, FF), FF ** -0.5, 0.09375, ((0, 2), (2, 4))),
        "w_ada": scatter_about(key_of[9], (LAYERS, D, 6 * D), D ** -0.5, 0.1875, ((0, 2),)),
        "ada_bias": scatter_about(key_of[10], (LAYERS, 6 * D), 0.5, 3.0, ((0, 2),)),
    }


@jax.custom_vjp
def low(v):
    return lax.optimization_barrier(v.astype(jnp.bfloat16)).astype(jnp.float32)

@jax.custom_vjp
def low_back(v):
    return v

def low_keep(v):
    return (low(v), None)

def low_pass(kept, grad):
    return (grad,)

def back_keep(v):
    return (v, None)

def back_low(kept, grad):
    return (low(grad),)
low.defvjp(low_keep, low_pass)
low_back.defvjp(back_keep, back_low)
precise = lax.Precision.HIGHEST

def norm_modulate(incoming_tokens, offset, factor):
    center = incoming_tokens - lax.optimization_barrier(jnp.mean(incoming_tokens, axis=-1, keepdims=True))
    spread = lax.optimization_barrier(jnp.mean(center * center, axis=-1, keepdims=True))
    return center * lax.rsqrt(spread + 1e-06) * (1.0 + factor) + offset

def modulations(cond_row, ada_weight, ada_shift):
    activated = low(jax.nn.silu(cond_row))
    return (jnp.dot(activated, ada_weight, precision=precise) + ada_shift).reshape(6, -1)

def diffusion_layer(incoming_tokens, modulation_rows, query_key_value_weight, query_value_bias, attention_output_weight, output_biases, first_mlp_weight, first_mlp_bias, second_mlp_weight):
    row_count = incoming_tokens.shape[0]
    normed = low(norm_modulate(incoming_tokens, modulation_rows[0], modulation_rows[1]))
    biases = jnp.stack([query_value_bias[0], jnp.zeros_like(query_value_bias[0]), query_value_bias[1]])
    triple = jnp.einsum('sd,dje->sje', normed, query_key_value_weight, precision=precise) + biases
    triple = low(low_back(triple)).reshape(row_count, 3, HEADS, HD)
    queries, key_rows, values = (triple[:, 0], triple[:, 1], triple[:, 2])
    scores = low_back(jnp.einsum('qhe,khe->hqk', queries, key_rows, precision=precise) * HD ** (-0.5))
    softmax_w = low(jax.nn.softmax(scores, axis=-1))
    mixed = jnp.einsum('hqk,khe->qhe', softmax_w, values, precision=precise).reshape(row_count, HEADS * HD)
    mixed = low(low_back(mixed))
    branch = low_back(jnp.dot(mixed, attention_output_weight.T, precision=precise) + output_biases[0])
    middle = incoming_tokens + modulation_rows[2] * branch
    second = low(norm_modulate(middle, modulation_rows[3], modulation_rows[4]))
    hidden_pre = low_back(jnp.dot(second, first_mlp_weight, precision=precise) + first_mlp_bias)
    activated = low(jax.nn.gelu(hidden_pre, approximate=True))
    feed = low_back(jnp.dot(activated, second_mlp_weight.T, precision=precise) + output_biases[1])
    return middle + modulation_rows[5] * feed

def latent_pass(incoming_tokens, cond_row, params):
    query_key_value_weight, query_value_bias, attention_output_weight, output_biases, first_mlp_weight, first_mlp_bias, second_mlp_weight, w_ada, ada_bias = params
    present_rows = incoming_tokens
    for layer_number in range(2):
        modulation_rows = modulations(cond_row, w_ada[layer_number], ada_bias[layer_number])
        present_rows = diffusion_layer(present_rows, modulation_rows, query_key_value_weight[layer_number], query_value_bias[layer_number], attention_output_weight[layer_number], output_biases[layer_number], first_mlp_weight[layer_number], first_mlp_bias[layer_number], second_mlp_weight[layer_number])
        if layer_number == 0:
            present_rows = low(low_back(present_rows))
    return present_rows

def forward(token_rows, cond_rows, params):
    single = jax.checkpoint(lambda incoming_tokens, cond_row: latent_pass(incoming_tokens, cond_row, params))
    return lax.map(lambda pair_rows: single(pair_rows[0], pair_rows[1]), (token_rows, cond_rows))

def reference(boundary, conditioning, query_key_value_weight, query_value_bias, attention_output_weight, output_biases, first_mlp_weight, first_mlp_bias, second_mlp_weight, w_ada, ada_bias):
    params = tuple((element.astype(jnp.float32) for element in (query_key_value_weight, query_value_bias, attention_output_weight, output_biases, first_mlp_weight, first_mlp_bias, second_mlp_weight, w_ada, ada_bias)))
    token_rows = boundary[0].astype(jnp.float32)
    cotangent = boundary[1].astype(jnp.float32)
    cond_rows = conditioning.astype(jnp.float32)
    result, pullback = jax.vjp(forward, token_rows, cond_rows, params)
    grad_tokens, grad_cond, grad_params = pullback(cotangent)
    ends = jnp.stack([grad_tokens, result]).astype(jnp.bfloat16)
    layer_count = query_key_value_weight.shape[0]
    return (ends, grad_cond, grad_params[0], grad_params[1].reshape(layer_count, -1), grad_params[2], grad_params[3].reshape(layer_count, -1), grad_params[4], grad_params[5], grad_params[6], grad_params[7], grad_params[8])
```

```python
import functools

import jax
import jax.numpy as jnp
from jax import lax
from jax.experimental import pallas as pl
from jax.experimental.pallas import tpu as pltpu
from jax.sharding import PartitionSpec as P

HD = 64
SLAB = 2 * HD
EXPO = HD ** (-0.5) * 1.4426950408889634
BF = jnp.bfloat16
F32 = jnp.float32
precise = lax.Precision.HIGHEST


def swap(block, bit):
    count = lax.axis_size("tensor")
    return lax.ppermute(block, "tensor", [(i, i ^ bit) for i in range(count)])


def tensor_sum(block):
    count = lax.axis_size("tensor")
    bit = 1
    while bit < count:
        block = block + swap(block, bit)
        bit *= 2
    return block


def call(kernel, ins, outs, scratch=(), token=None, flag=None, flops=0):
    vmem = pl.BlockSpec(memory_space=pltpu.VMEM)
    specs = [vmem] * len(ins)
    if flag is not None:
        ins = (flag, *ins)
        specs = [pl.BlockSpec(memory_space=pltpu.SMEM), *specs]
    body = kernel
    if token is not None:
        token = token if isinstance(token, tuple) else (token,)
        place = len(ins)
        ins = (*ins, *token)
        specs += [pl.BlockSpec(memory_space=pl.ANY)] * len(token)

        def body(*refs):
            kernel(*refs[:place], *refs[len(ins) :])

    return pl.pallas_call(
        body,
        in_specs=specs,
        out_specs=[vmem] * len(outs),
        out_shape=list(outs),
        scratch_shapes=list(scratch),
        compiler_params=pltpu.CompilerParams(vmem_limit_bytes=24 << 20),
        cost_estimate=pl.CostEstimate(flops=flops, bytes_accessed=0, transcendentals=0),
    )(*ins)


def like(rows, cols, kind):
    return jax.ShapeDtypeStruct((rows, cols), kind)


def dot_nn(left, right):
    return jnp.dot(left, right, preferred_element_type=F32)


def dot_nt(left, right):
    return lax.dot_general(left, right, (((1,), (1,)), ((), ())), preferred_element_type=F32)


def unit_rows(rows):
    center = rows - jnp.mean(rows, axis=-1, keepdims=True)
    spread = jnp.mean(center * center, axis=-1, keepdims=True)
    inverse = lax.rsqrt(spread + 1e-06)
    return center * inverse, inverse


def norm_back(unit, inverse, grad, factor):
    grad_unit = grad * (1.0 + factor)
    return inverse * (
        grad_unit
        - jnp.mean(grad_unit, axis=-1, keepdims=True)
        - unit * jnp.mean(grad_unit * unit, axis=-1, keepdims=True)
    )


def gelu_both(u):
    root = 0.7978845608028654
    square = u * u
    inner = root * (1.0 + 0.044715 * square)
    tanh = jnp.tanh(u * inner)
    half = 0.5 * (1.0 + tanh)
    slope = half + (0.5 * u) * (1.0 - tanh * tanh) * (root + (3.0 * 0.044715 * root) * square)
    return u * half, slope


def total(ref):
    return jnp.sum(ref, axis=0, keepdims=True)


def first_norm_kernel(rows_ref, mod_ref, out_ref):
    unit, _ = unit_rows(rows_ref[...].astype(F32))
    out_ref[...] = (unit * (1.0 + mod_ref[1:2]) + mod_ref[0:1]).astype(BF)


def triple_kernel(rows_ref, own_w_ref, other_w_ref, bias_ref, triple_ref, *send_refs):
    width = own_w_ref.shape[1]
    third = width // 3
    for group, w_ref in enumerate((own_w_ref, other_w_ref)):
        cols = slice(group * width, (group + 1) * width)
        part = (dot_nn(rows_ref[...], w_ref[...]) + bias_ref[:, cols]).astype(BF)
        triple_ref[:, cols] = part
        send_refs[1 - group][...] = part[:, third:]


def slabs(width):
    return [(group, first) for group in range(2) for first in range(0, width, SLAB)]


def key_blocks(near_ref, far_ref, away_near_ref, away_far_ref, group, first, width, which):
    here = group * 3 * width + which * width + first
    away = (which - 1) * width + first
    return [ref[:, here : here + SLAB] for ref in (near_ref, far_ref)] + [
        refs[group][:, away : away + SLAB] for refs in (away_near_ref, away_far_ref)
    ]


def sum_of(terms):
    return functools.reduce(lambda one, two: one + two, terms)


def attend_kernel(
    query_ref, near_ref, far_ref, an0_ref, an1_ref, af0_ref, af1_ref, own_w_ref, other_w_ref, mixed_ref, log_ref, out_ref
):
    away_near_ref, away_far_ref = (an0_ref, an1_ref), (af0_ref, af1_ref)
    block = mixed_ref.shape[0]
    width = mixed_ref.shape[1] // 2
    upper = lax.broadcasted_iota(jnp.int32, (SLAB, block), 0) >= HD
    for group, first in slabs(width):
        start = group * 3 * width + first
        queries = query_ref[:, start : start + SLAB].T
        tokens = (near_ref, far_ref, away_near_ref, away_far_ref, group, first, width)
        keys = key_blocks(*tokens, 1)
        values = [part.T for part in key_blocks(*tokens, 2)]
        outs = []
        for h in range(2):
            part = jnp.where(upper == (h == 1), queries, jnp.zeros_like(queries))
            scores = [dot_nn(key, part) for key in keys]
            peak = functools.reduce(jnp.maximum, [jnp.max(x, axis=0, keepdims=True) for x in scores])
            expo = [jnp.exp2((x - peak) * EXPO) for x in scores]
            weight = sum_of([total(x) for x in expo])
            out = sum_of(
                [dot_nn(value[h * HD : (h + 1) * HD], x.astype(BF)) for value, x in zip(values, expo)]
            )
            outs.append(out * (1.0 / weight))
            head = (group * width + first) // HD + h
            log_ref[head : head + 1, :] = peak * EXPO + jnp.log2(weight)
        at = group * width + first
        mixed_ref[:, at : at + SLAB] = jnp.concatenate(outs, 0).T.astype(BF)
    branch = dot_nt(mixed_ref[:, :width], own_w_ref[...]) + dot_nt(mixed_ref[:, width:], other_w_ref[...])
    out_ref[...] = branch.astype(out_ref.dtype)


def middle_kernel(keep_ref, far_ref, bias_ref, rows_ref, mod_ref, branch_ref, middle_ref, second_ref):
    branch = keep_ref[...] + far_ref[...].astype(F32) + bias_ref[...]
    middle = rows_ref[...].astype(F32) + mod_ref[2:3] * branch
    unit, _ = unit_rows(middle)
    branch_ref[...] = branch
    middle_ref[...] = middle
    second_ref[...] = (unit * (1.0 + mod_ref[4:5]) + mod_ref[3:4]).astype(BF)


def mlp_kernel(rows_ref, own_w1_ref, other_w1_ref, bias_ref, own_w2_ref, other_w2_ref, act_ref, slope_ref, out_ref):
    width = own_w1_ref.shape[1]
    tile = 256
    for group, w1_ref in enumerate((own_w1_ref, other_w1_ref)):
        for first in range(0, width, tile):
            cols = slice(group * width + first, group * width + first + tile)
            value, slope = gelu_both(dot_nn(rows_ref[...], w1_ref[:, first : first + tile]) + bias_ref[:, cols])
            act_ref[:, cols] = value.astype(BF)
            slope_ref[:, cols] = slope.astype(BF)
    feed = dot_nt(act_ref[:, :width], own_w2_ref[...]) + dot_nt(act_ref[:, width:], other_w2_ref[...])
    out_ref[...] = feed.astype(out_ref.dtype)


def layer_end_kernel(keep_ref, far_ref, bias_ref, middle_ref, mod_ref, feed_ref, out_ref):
    feed = keep_ref[...] + far_ref[...].astype(F32) + bias_ref[...]
    feed_ref[...] = feed
    out_ref[...] = (middle_ref[...] + mod_ref[5:6] * feed).astype(BF)


def grad_feed_kernel(grad_ref, feed_ref, mod_ref, out_ref, sums_ref):
    grad = grad_ref[...].astype(F32)
    out = (mod_ref[5:6] * grad).astype(BF)
    out_ref[...] = out
    sums_ref[0:1] = total(grad * feed_ref[...])
    sums_ref[1:2] = total(out.astype(F32))


def grad_mlp_kernel(rows_ref, own_w2_ref, other_w2_ref, slope_ref, own_w1_ref, other_w1_ref, hidden_ref, sums_ref, out_ref):
    width = own_w2_ref.shape[1]
    tile = 256
    for group, w2_ref in enumerate((own_w2_ref, other_w2_ref)):
        for first in range(0, width, tile):
            cols = slice(group * width + first, group * width + first + tile)
            grad = dot_nn(rows_ref[...], w2_ref[:, first : first + tile])
            grad = (grad * slope_ref[:, cols].astype(F32)).astype(BF)
            hidden_ref[:, cols] = grad
            sums_ref[:, cols] = total(grad.astype(F32))
    second = dot_nt(hidden_ref[:, :width], own_w1_ref[...]) + dot_nt(hidden_ref[:, width:], other_w1_ref[...])
    out_ref[...] = second.astype(out_ref.dtype)


def grad_middle_kernel(keep_ref, far_ref, middle_ref, branch_ref, grad_ref, mod_ref, out_ref, rows_ref, sums_ref):
    grad = keep_ref[...] + far_ref[...].astype(F32)
    unit, inverse = unit_rows(middle_ref[...])
    sums_ref[0:1] = total(grad)
    sums_ref[1:2] = total(grad * unit)
    grad = norm_back(unit, inverse, grad, mod_ref[4:5]) + grad_ref[...].astype(F32)
    out_ref[...] = grad
    sums_ref[2:3] = total(grad * branch_ref[...])
    rows = (mod_ref[2:3] * grad).astype(BF)
    rows_ref[...] = rows
    sums_ref[3:4] = total(rows.astype(F32))


def grad_attend_kernel(last, *refs):
    rows_ref, own_w_ref, other_w_ref, query_ref, near_ref, far_ref = refs[:6]
    away_near_ref, away_far_ref = refs[6:8], refs[8:10]
    mixed_ref, log_ref = refs[10:12]
    if last:
        held_ref, out_ref, keep_ref, send_ref, grad_ref = refs[12:]
    else:
        out_ref, keep_ref, grad_ref = refs[12:]
    block = mixed_ref.shape[0]
    width = mixed_ref.shape[1] // 2
    scale = HD ** (-0.5)
    for group, w_ref in enumerate((own_w_ref, other_w_ref)):
        grad_ref[:, group * width : (group + 1) * width] = dot_nn(rows_ref[...], w_ref[...]).astype(BF)
    upper = lax.broadcasted_iota(jnp.int32, (SLAB, block), 0) >= HD
    right = lax.broadcasted_iota(jnp.int32, (block, SLAB), 1) >= HD
    for group, first in slabs(width):
        at = group * width + first
        start = group * 3 * width + first
        queries = query_ref[:, start : start + SLAB]
        grad = grad_ref[:, at : at + SLAB]
        queries_t, grad_t = queries.T, grad.T
        tokens = (near_ref, far_ref, away_near_ref, away_far_ref, group, first, width)
        inner = grad_t.astype(F32) * mixed_ref[:, at : at + SLAB].T.astype(F32)
        none = jnp.zeros_like(queries_t)
        none_r = jnp.zeros_like(queries)
        heads = []
        for h in range(2):
            heads.append(
                (
                    jnp.where(upper == (h == 1), queries_t, none),
                    jnp.where(upper == (h == 1), grad_t, none),
                    jnp.where(right == (h == 1), queries, none_r),
                    jnp.where(right == (h == 1), grad, none_r),
                    total(inner[h * HD : (h + 1) * HD]),
                )
            )
        outs = [None, None]
        for place, (keys, values) in enumerate(zip(key_blocks(*tokens, 1), key_blocks(*tokens, 2))):
            keys_t = keys.T
            key_terms, value_terms = [], []
            for h, (query_t, grad_out_t, query, grad_out, delta) in enumerate(heads):
                head = at // HD + h
                probs = jnp.exp2(dot_nn(keys, query_t) * EXPO - log_ref[head : head + 1, :])
                grad_s = (probs * (dot_nn(values, grad_out_t) - delta)).astype(BF)
                value_terms.append(dot_nn(probs.astype(BF), grad_out))
                key_terms.append(dot_nn(grad_s, query))
                out = dot_nn(keys_t[h * HD : (h + 1) * HD], grad_s)
                outs[h] = out if outs[h] is None else outs[h] + out
            for which, term in enumerate((sum_of(key_terms) * scale, sum_of(value_terms))):
                rows = slice(place * block, (place + 1) * block)
                cols = slice(group * 2 * width + which * width + first, group * 2 * width + which * width + first + SLAB)
                if not last:
                    keep_ref[rows, cols] = term
                elif place < 2:
                    keep_ref[rows, cols] = held_ref[rows, cols] + term
                else:
                    there = slice((place - 2) * block, (place - 1) * block)
                    turned = (1 - group) * 2 * width + which * width + first
                    send_ref[there, turned : turned + SLAB] = (held_ref[rows, cols] + term).astype(BF)
        out_ref[:, at : at + SLAB] = (jnp.concatenate(outs, 0).T * scale).astype(BF)


def grad_normed_kernel(part, query_ref, keep_ref, got_ref, own_w_ref, other_w_ref, triple_ref, out_ref, sums_ref):
    size, width = query_ref.shape[0], query_ref.shape[1] // 2
    rows = slice(part * size, (part + 1) * size)
    for group in range(2):
        at = group * 3 * width
        cols = slice(group * 2 * width, (group + 1) * 2 * width)
        triple_ref[:, at : at + width] = query_ref[:, group * width : (group + 1) * width]
        triple_ref[:, at + width : at + 3 * width] = (
            keep_ref[rows, cols] + got_ref[rows, cols].astype(F32)
        ).astype(BF)
    out = dot_nt(triple_ref[:, : 3 * width], own_w_ref[...]) + dot_nt(triple_ref[:, 3 * width :], other_w_ref[...])
    out_ref[...] = out.astype(out_ref.dtype)
    sums_ref[...] = total(triple_ref[...].astype(F32))


def grad_rows_kernel(keep_ref, far_ref, rows_ref, middle_ref, mod_ref, out_ref, sums_ref):
    grad = keep_ref[...] + far_ref[...].astype(F32)
    unit, inverse = unit_rows(rows_ref[...].astype(F32))
    sums_ref[0:1] = total(grad)
    sums_ref[1:2] = total(grad * unit)
    out_ref[...] = (norm_back(unit, inverse, grad, mod_ref[1:2]) + middle_ref[...]).astype(BF)


CHUNKS = 4


def weight_kernel(lefts, rights, wanted, flag_ref, *refs):
    left_refs, right_refs = refs[:lefts], refs[lefts : lefts + rights]
    rest = refs[lefts + rights : -2]
    left_all, right_all = refs[-2:]
    out_refs = rest[-1 - CHUNKS :]

    @pl.when(flag_ref[0] == wanted)
    def _():
        at = 0
        for ref in left_refs:
            left_all[:, at : at + ref.shape[0]] = ref[...].T
            at += ref.shape[0]
        at = 0
        for ref in right_refs:
            right_all[at : at + ref.shape[0]] = ref[...]
            at += ref.shape[0]
        rows, width = out_refs[0].shape
        tile = rows // CHUNKS
        for i in range(CHUNKS):
            left = left_all[i * tile : (i + 1) * tile]
            out_refs[0][i * tile : (i + 1) * tile] = dot_nn(left, right_all[:, :width]).astype(BF)
            out_refs[i + 1][...] = dot_nn(left, right_all[:, width:]).astype(BF)

    @pl.when(flag_ref[0] != wanted)
    def _():
        for i, out_ref in enumerate(out_refs):
            out_ref[...] = jnp.zeros_like(out_ref) if len(rest) == len(out_refs) else rest[i][...]


def weight_grad(operands, section, old, token):
    lefts, rights = operands
    tokens = sum(x.shape[0] for x in lefts)
    rows, cols = lefts[0].shape[1], rights[0].shape[1]
    return call(
        functools.partial(weight_kernel, len(lefts), len(rights), 1 if old is None else 0),
        (*lefts, *rights) if old is None else (*lefts, *rights, *old),
        [like(rows, cols // 2, BF)] + [like(rows // CHUNKS, cols // 2, BF)] * CHUNKS,
        scratch=[pltpu.VMEM((rows, tokens), BF), pltpu.VMEM((tokens, cols), BF)],
        token=token,
        flag=section,
    )


def add_kernel(one_ref, *refs):
    out_ref = refs[-1]
    size = out_ref.shape[0] // CHUNKS
    for i, two_ref in enumerate(refs[:-1]):
        rows = slice(i * size, (i + 1) * size)
        out_ref[rows] = (one_ref[rows].astype(F32) + two_ref[...].astype(F32)).astype(BF)


def tied(block, token):
    if token is None:
        return block
    token = token if isinstance(token, tuple) else (token,)
    return lax.optimization_barrier((block, *token))[0]


def forward_steps(rows, mod, weights):
    w_qkv, b_qkv, w_out, b_out, w_fc1, b_fc1, w_fc2 = weights
    size, width = rows.shape
    local = w_out[0].shape[1]
    hidden = w_fc1[0].shape[1]
    token = yield None, ()
    (normed,) = call(first_norm_kernel, (rows, mod), [like(size, width, BF)], token=token)
    normed_far = swap(normed, 2)
    triple_outs = [like(size, 6 * local, BF), like(size, 2 * local, BF), like(size, 2 * local, BF)]
    triple, *sends = call(triple_kernel, (normed, *w_qkv, b_qkv), triple_outs)
    away = [swap(send, 1) for send in sends]
    token = yield triple, ()
    normed_far = tied(normed_far, token)
    triple_far, *sends = call(triple_kernel, (normed_far, *w_qkv, b_qkv), triple_outs, token=token)
    tokens = (triple, triple_far, *away, *(swap(send, 1) for send in sends))
    outs = [like(size, 2 * local, BF), like(2 * local // HD, size, F32)]
    mixed_far, log_far, send = call(
        attend_kernel, (triple_far, *tokens, *w_out), [*outs, like(size, width, BF)], token=token
    )
    far = swap(send, 2)
    mixed, log, keep = call(
        attend_kernel, (triple, *tokens, *w_out), [*outs, like(size, width, F32)], token=send
    )
    token = yield keep, ()
    branch, middle, second = call(
        middle_kernel,
        (keep, tied(far, token), b_out[0:1], rows, mod),
        [like(size, width, F32), like(size, width, F32), like(size, width, BF)],
        token=token,
    )
    second_far = swap(second, 2)
    outs = [like(size, 2 * hidden, BF), like(size, 2 * hidden, BF)]
    act, slope, keep = call(mlp_kernel, (second, *w_fc1, b_fc1, *w_fc2), [*outs, like(size, width, F32)])
    token = yield keep, ()
    second_far = tied(second_far, token)
    act_far, slope_far, send = call(
        mlp_kernel, (second_far, *w_fc1, b_fc1, *w_fc2), [*outs, like(size, width, BF)], token=token
    )
    far = swap(send, 2)
    token = yield send, ()
    feed, result = call(
        layer_end_kernel,
        (keep, tied(far, token), b_out[1:2], middle, mod),
        [like(size, width, F32), like(size, width, BF)],
        token=token,
    )
    state = (
        rows, (normed, normed_far), tokens, (mixed, mixed_far), (log, log_far), branch, middle,
        (second, second_far), (act, act_far), (slope, slope_far), feed,
    )
    return result, state


def backward_steps(grad, mod, weights, state, flops=0):
    w_qkv, b_qkv, w_out, b_out, w_fc1, b_fc1, w_fc2 = weights
    rows, normed, tokens, mixed, logs, branch, middle, second, acts, slopes, feed = state
    size, width = rows.shape
    local = w_out[0].shape[1]
    hidden = w_fc1[0].shape[1]
    token = yield None, ()
    feed_rows, sums_feed = call(
        grad_feed_kernel, (grad, feed, mod), [like(size, width, BF), like(2, width, F32)], token=token
    )
    feed_far = swap(feed_rows, 2)
    outs = [like(size, 2 * hidden, BF), like(1, 2 * hidden, F32)]
    hidden_near, sums_near, keep = call(
        grad_mlp_kernel, (feed_rows, *w_fc2, slopes[0], *w_fc1), [*outs, like(size, width, F32)]
    )
    token = yield keep, ()
    feed_far = tied(feed_far, token)
    hidden_far, sums_far, send = call(
        grad_mlp_kernel, (feed_far, *w_fc2, slopes[1], *w_fc1), [*outs, like(size, width, BF)], token=token
    )
    far = swap(send, 2)
    token = yield send, ((3, (feed_rows, feed_far), acts),)
    grad_middle, branch_rows, sums_middle = call(
        grad_middle_kernel,
        (keep, tied(far, token), middle, branch, grad, mod),
        [like(size, width, F32), like(size, width, BF), like(4, width, F32)],
        token=token,
    )
    branch_far = swap(branch_rows, 2)
    scratch = [pltpu.VMEM((size, 2 * local), BF)]
    query_near, held = call(
        functools.partial(grad_attend_kernel, False),
        (branch_rows, *w_out, tokens[0], *tokens, mixed[0], logs[0]),
        [like(size, 2 * local, BF), like(4 * size, 4 * local, F32)],
        scratch=scratch,
    )
    token = yield query_near, ((2, second, (hidden_near, hidden_far)),)
    branch_far = tied(branch_far, token)
    query_far, kept, send = call(
        functools.partial(grad_attend_kernel, True),
        (branch_far, *w_out, tokens[1], *tokens, mixed[1], logs[1], held),
        [like(size, 2 * local, BF), like(2 * size, 4 * local, F32), like(2 * size, 4 * local, BF)],
        scratch=scratch,
        token=token,
        flops=flops,
    )
    got = swap(send, 1)
    token = yield kept, ((1, (branch_rows, branch_far), mixed),)
    outs = [like(size, 6 * local, BF), like(size, width, BF), like(1, 6 * local, F32)]
    triple_far, send, sums_triple_far = call(
        functools.partial(grad_normed_kernel, 1), (query_far, kept, got, *w_qkv), outs, token=token
    )
    far = swap(send, 2)
    outs[1] = like(size, width, F32)
    triple_near, keep, sums_triple = call(
        functools.partial(grad_normed_kernel, 0), (query_near, kept, got, *w_qkv), outs, token=send
    )
    token = yield keep, ((0, normed, (triple_near, triple_far)),)
    grad_rows, sums_rows = call(
        grad_rows_kernel,
        (keep, tied(far, token), rows, grad_middle, mod),
        [like(size, width, BF), like(2, width, F32)],
        token=token,
    )
    grad_mod = jnp.concatenate(
        [sums_rows, sums_middle[2:3], sums_middle[0:2], sums_feed[0:1]], 0
    ).reshape(1, -1)
    sums = (
        (sums_triple + sums_triple_far)[0],
        (sums_near + sums_far)[0],
        jnp.concatenate([sums_middle[3:4], sums_feed[1:2]], 0),
    )
    return grad_rows, grad_mod, sums


def chain_steps(ends, mod, weights, flops):
    sent, state_one = yield from forward_steps(ends, mod, weights)
    arrived = lax.ppermute(sent, "section", [(0, 1)])
    yield sent, ()
    out, state_two = yield from forward_steps(arrived, mod, weights)
    yield out, ()
    back_two = yield from backward_steps(ends, mod, weights, state_two)
    arrived = lax.ppermute(back_two[0], "section", [(1, 0)])
    yield back_two[0], ()
    back_one = yield from backward_steps(arrived, mod, weights, state_one, flops)
    yield back_one[0], ()
    return out, back_two, back_one


def side_by_side(chains, section):
    results = [None] * len(chains)
    products, sums, pending = {}, {}, []
    after = {0: 2}
    for chain in chains:
        next(chain)
    token = None
    while pending or any(result is None for result in results):
        ready = {}
        if any(which == 0 for which, _, _ in pending):
            token = (token, sums[3])
        for i, chain in enumerate(chains):
            try:
                token, made = chain.send(token)
            except StopIteration as stop:
                results[i] = stop.value
                continue
            for which, lefts, rights in made:
                both = ready.setdefault(which, ([], []))
                both[0].extend(lefts)
                both[1].extend(rights)
        for which, keep, got in pending:
            if which in after:
                token = (token, sums[after[which]])
            (token,) = call(add_kernel, (keep, *got), [like(*keep.shape, BF)], token=token)
            sums[which] = lax.psum_scatter(token, "dp", scatter_dimension=0, tiled=True)
        pending = []
        for which, operands in ready.items():
            old = products.get(which)
            products[which] = keep, *sends = weight_grad(operands, section, old, token)
            token = keep
            if old is not None:
                pending.append((which, keep, [swap(send, 1) for send in sends]))
    return results, sums


def body(
    boundary,
    conditioning,
    query_key_value_weight,
    query_value_bias,
    attention_output_weight,
    output_biases,
    first_mlp_weight,
    first_mlp_bias,
    second_mlp_weight,
    w_ada,
    ada_bias,
):
    leading = lax.axis_index("section") == 0
    ends = boundary[0]
    width, _, local = query_key_value_weight.shape[1:]
    tensor_no = lax.axis_index("tensor")
    dp_no = lax.axis_index("dp")
    tensor_count = lax.axis_size("tensor")
    dp_count = lax.axis_size("dp")
    w_qkv = jnp.concatenate([query_key_value_weight[0, :, i] for i in range(3)], 1)
    qv = query_value_bias[0].astype(F32)
    b_qkv = jnp.concatenate([qv[0], jnp.zeros_like(qv[0]), qv[1]])[None]
    w_out, w_fc1, w_fc2 = attention_output_weight[0], first_mlp_weight[0], second_mlp_weight[0]
    hidden = w_fc1.shape[1]
    vectors = jnp.concatenate([b_qkv, first_mlp_bias.astype(F32)], 1)
    other = swap(vectors, 1)
    weights = (
        (w_qkv, swap(w_qkv, 1)),
        jnp.concatenate([b_qkv, other[:, : 3 * local]], 1),
        (w_out, swap(w_out, 1)),
        output_biases[0].astype(F32),
        (w_fc1, swap(w_fc1, 1)),
        jnp.concatenate([vectors[:, 3 * local :], other[:, 3 * local :]], 1),
        (w_fc2, swap(w_fc2, 1)),
    )
    ada_weight = w_ada[0]
    cond_vals = conditioning.astype(F32)
    cond_act = jax.nn.silu(cond_vals).astype(BF)
    mods = (dot_nn(cond_act, ada_weight) + ada_bias[0].astype(F32)).reshape(2, 6, width)

    section = lax.axis_index("section").astype(jnp.int32).reshape(1)
    chains, sums = side_by_side(
        [chain_steps(ends[b], mods[b], weights, b * 10**11) for b in range(ends.shape[0])], section
    )
    outs = [chain[0] for chain in chains]
    backs_two = [chain[1] for chain in chains]
    backs_one = [chain[2] for chain in chains]

    g_qkv, g_proj, g_fc1, g_fc2 = (sums[i].astype(F32) for i in range(4))
    g_qkv = jnp.stack([g_qkv[:, i * local : (i + 1) * local] for i in range(3)], 1)

    pick = lambda one, two: jnp.where(leading, one, two)
    grad_mods = jnp.concatenate(
        [pick(one[1], two[1]) for one, two in zip(backs_one, backs_two)], 0
    )
    owned_triple, owned_hidden, partial = (
        pick(
            backs_one[0][2][i] + backs_one[1][2][i],
            backs_two[0][2][i] + backs_two[1][2][i],
        )
        for i in range(3)
    )
    def placed(vector):
        size = vector.shape[0] // 2
        full = jnp.zeros((tensor_count * size,), F32)
        for part, where in ((vector[:size], tensor_no), (vector[size:], tensor_no ^ 1)):
            full = lax.dynamic_update_slice(full, part, (where * size,))
        return full

    span = 3 * local
    queries = jnp.concatenate([owned_triple[:local], owned_triple[span : span + local]])
    values = jnp.concatenate([owned_triple[2 * local : span], owned_triple[span + 2 * local :]])
    flat = tensor_sum(
        jnp.concatenate(
            [
                grad_mods.reshape(-1),
                placed(queries),
                placed(values),
                placed(owned_hidden),
                partial.reshape(-1),
            ]
        )
    )
    grad_mods = flat[: 12 * width].reshape(2, 6 * width)
    biases = flat[12 * width :]
    everything = lax.all_gather(
        jnp.concatenate([grad_mods.reshape(-1), biases, cond_act.astype(F32).reshape(-1)]), "dp", axis=0
    )
    mods_end = 12 * width
    all_mods = everything[:, :mods_end].reshape(2 * dp_count, 6 * width)
    all_acts = everything[:, -2 * width :].reshape(2 * dp_count, width)
    biases = jnp.sum(everything[:, mods_end : -2 * width], axis=0)
    place = dp_no * tensor_count + tensor_no
    shares = dp_count * tensor_count

    def own_share(vector):
        size = vector.shape[0] // shares
        return lax.dynamic_slice(vector, (place * size,), (size,))[None]

    hidden_all = biases.shape[0] - 4 * width
    g_qv_bias = own_share(biases[: 2 * width])
    g_fc1_bias = own_share(biases[2 * width : 2 * width + hidden_all])
    g_out_bias = own_share(biases[2 * width + hidden_all :])
    g_ada_bias = own_share(jnp.sum(all_mods, axis=0))
    share = width // shares
    act_share = lax.dynamic_slice(all_acts, (0, place * share), (all_acts.shape[0], share))
    g_ada = lax.dot_general(
        act_share, all_mods, (((0,), (0,)), ((), ())), precision=precise, preferred_element_type=F32
    )

    cut = 6 * width // tensor_count
    mods_cut = lax.dynamic_slice(grad_mods, (0, tensor_no * cut), (2, cut))
    ada_cut = lax.dynamic_slice(ada_weight, (0, tensor_no * cut), (width, cut))
    back_cond = lax.dot_general(
        mods_cut,
        ada_cut.astype(F32),
        (((1,), (1,)), ((), ())),
        precision=precise,
        preferred_element_type=F32,
    )
    back_cond = back_cond + lax.ppermute(back_cond, "section", [(0, 1), (1, 0)])
    cond_total = tensor_sum(back_cond)
    sig = jax.nn.sigmoid(cond_vals)
    cond_grad = cond_total * sig * (1.0 + cond_vals * (1.0 - sig))

    rows_out = jnp.stack([pick(back[0], out) for back, out in zip(backs_one, outs)])[None]
    return (
        rows_out,
        cond_grad,
        g_qkv[None],
        g_qv_bias,
        g_proj[None],
        g_out_bias,
        g_fc1[None],
        g_fc1_bias,
        g_fc2[None],
        g_ada[None],
        g_ada_bias,
    )


def solution(mesh):
    in_specs = (
        P("section", "dp", "tensor", None),
        P("dp", None),
        P("section", None, None, "tensor"),
        P("section", None, "tensor"),
        P("section", None, "tensor"),
        P("section", None, None),
        P("section", None, "tensor"),
        P("section", "tensor"),
        P("section", None, "tensor"),
        P("section", None, None),
        P("section", None),
    )
    out_specs = (
        P("section", "dp", "tensor", None),
        P("dp", None),
        P("section", "dp", None, "tensor"),
        P("section", ("dp", "tensor")),
        P("section", "dp", "tensor"),
        P("section", ("dp", "tensor")),
        P("section", "dp", "tensor"),
        P("section", ("dp", "tensor")),
        P("section", "dp", "tensor"),
        P("section", ("dp", "tensor"), None),
        P("section", ("dp", "tensor")),
    )
    return jax.shard_map(body, mesh=mesh, in_specs=in_specs, out_specs=out_specs, check_vma=False)
```

```python
import functools

import jax
import jax.numpy as jnp
from jax import lax
from jax.experimental import pallas as pl
from jax.experimental.pallas import tpu as pltpu
from jax.sharding import PartitionSpec as P

HD = 64
SLAB = 2 * HD
EXPO = HD ** (-0.5) * 1.4426950408889634
BF = jnp.bfloat16
F32 = jnp.float32
precise = lax.Precision.HIGHEST


def swap(block, bit):
    count = lax.axis_size("tensor")
    return lax.ppermute(block, "tensor", [(i, i ^ bit) for i in range(count)])


def tensor_sum(block):
    count = lax.axis_size("tensor")
    bit = 1
    while bit < count:
        block = block + swap(block, bit)
        bit *= 2
    return block


TIMES = {
    "first_norm_kernel": 1,
    "triple_kernel": 3,
    "attend_kernel": 8,
    "middle_kernel": 1,
    "mlp_kernel": 6,
    "layer_end_kernel": 1,
    "grad_feed_kernel": 1,
    "grad_mlp_kernel": 6,
    "grad_middle_kernel": 2,
    "grad_attend_kernel": 11,
    "grad_normed_kernel": 3,
    "grad_rows_kernel": 1,
    "weight_kernel": 6,
    "add_kernel": 1,
    "copy_kernel": 1,
}
SHARE = 1


def over_dp(block):
    count = lax.axis_size("dp")
    if count & (count - 1):
        return lax.all_gather(block, "dp", axis=0, tiled=True)
    bit = 1
    while bit < count:
        other = lax.ppermute(block, "dp", [(i, i ^ bit) for i in range(count)])
        block = jnp.concatenate([block, other], 0)
        bit *= 2
    return block


def line_reduce(block):
    count, place = lax.axis_size("dp"), lax.axis_index("dp")
    size = block.shape[0] // count

    def chunk(owner):
        at = jnp.clip(owner, 0, count - 1) * size
        return lax.dynamic_slice(block, (at, 0), (size, block.shape[1])).astype(F32)

    came = []
    up = down = jnp.zeros((size, block.shape[1]), BF)
    for step in range(1, count):
        up = (chunk(place + count - step) + up.astype(F32)).astype(BF)
        down = (chunk(place - count + step) + down.astype(F32)).astype(BF)
        up, down = lax.optimization_barrier((up, down))
        up = lax.ppermute(up, "dp", [(i, i + 1) for i in range(step)])
        down = lax.ppermute(down, "dp", [(i, i - 1) for i in range(count - step, count)])
        came.append((up, down))
    return chunk(place) + up.astype(F32) + down.astype(F32), came


def call(kernel, ins, outs, scratch=(), token=None, flag=None, flops=0, far_in=(), far_out=()):
    name = getattr(kernel, "func", kernel).__name__
    vmem = pl.BlockSpec(memory_space=pltpu.VMEM)
    anywhere = pl.BlockSpec(memory_space=pl.ANY)
    specs = [anywhere if i in far_in else vmem for i in range(len(ins))]
    if flag is not None:
        ins = (flag, *ins)
        specs = [pl.BlockSpec(memory_space=pltpu.SMEM), *specs]
    body = kernel
    if token is not None:
        token = token if isinstance(token, tuple) else (token,)
        place = len(ins)
        ins = (*ins, *token)
        specs += [anywhere] * len(token)

        def body(*refs):
            kernel(*refs[:place], *refs[len(ins) :])

    shift = 0 if flag is None else 1
    ins = [outside(x) if i - shift in far_in else x for i, x in enumerate(ins)]
    results = pl.pallas_call(
        body,
        in_specs=specs,
        out_specs=[anywhere if i in far_out else vmem for i in range(len(outs))],
        out_shape=list(outs),
        scratch_shapes=list(scratch),
        compiler_params=pltpu.CompilerParams(vmem_limit_bytes=(20 if name == "weight_kernel" else 14) << 20),
        cost_estimate=pl.CostEstimate(flops=flops or int(TIMES[name] * SHARE * 1.15e9), bytes_accessed=0, transcendentals=0),
    )(*ins)
    return [outside(x) if i in far_out else x for i, x in enumerate(results)]


def outside(block):
    return pltpu.with_memory_space_constraint(block, pltpu.HBM)


def like(rows, cols, kind):
    return jax.ShapeDtypeStruct((rows, cols), kind)


def dot_nn(left, right):
    return jnp.dot(left, right, preferred_element_type=F32)


def dot_nt(left, right):
    return lax.dot_general(left, right, (((1,), (1,)), ((), ())), preferred_element_type=F32)


def unit_rows(rows):
    center = rows - jnp.mean(rows, axis=-1, keepdims=True)
    spread = jnp.mean(center * center, axis=-1, keepdims=True)
    inverse = lax.rsqrt(spread + 1e-06)
    return center * inverse, inverse


def norm_back(unit, inverse, grad, factor):
    grad_unit = grad * (1.0 + factor)
    return inverse * (
        grad_unit
        - jnp.mean(grad_unit, axis=-1, keepdims=True)
        - unit * jnp.mean(grad_unit * unit, axis=-1, keepdims=True)
    )


def gelu_both(u):
    root = 0.7978845608028654
    square = u * u
    inner = root * (1.0 + 0.044715 * square)
    tanh = jnp.tanh(u * inner)
    half = 0.5 * (1.0 + tanh)
    slope = half + (0.5 * u) * (1.0 - tanh * tanh) * (root + (3.0 * 0.044715 * root) * square)
    return u * half, slope


def total(ref):
    return jnp.sum(ref, axis=0, keepdims=True)


def first_norm_kernel(rows_ref, mod_ref, out_ref):
    unit, _ = unit_rows(rows_ref[...].astype(F32))
    out_ref[...] = (unit * (1.0 + mod_ref[1:2]) + mod_ref[0:1]).astype(BF)


def triple_kernel(rows_ref, own_w_ref, other_w_ref, bias_ref, triple_ref, *send_refs):
    width = own_w_ref.shape[1]
    third = width // 3
    for group, w_ref in enumerate((own_w_ref, other_w_ref)):
        cols = slice(group * width, (group + 1) * width)
        part = (dot_nn(rows_ref[...], w_ref[...]) + bias_ref[:, cols]).astype(BF)
        triple_ref[:, cols] = part
        send_refs[1 - group][...] = part[:, third:]


def slabs(width):
    return [(group, first) for group in range(2) for first in range(0, width, SLAB)]


def tokens_of(near_ref, far_ref, away_near_ref, away_far_ref, group, first, width, which):
    here = group * 3 * width + which * width + first
    away = (which - 1) * width + first
    return jnp.concatenate(
        [ref[:, here : here + SLAB] for ref in (near_ref, far_ref)]
        + [refs[group][:, away : away + SLAB] for refs in (away_near_ref, away_far_ref)],
        0,
    )


def queries_of(near_ref, far_ref, group, first, width):
    start = group * 3 * width + first
    return jnp.concatenate([ref[:, start : start + SLAB] for ref in (near_ref, far_ref)], 0)


def attend_kernel(
    near_ref, far_ref, an0_ref, an1_ref, af0_ref, af1_ref, own_w_ref, other_w_ref, mixed_ref, log_ref, keep_ref, send_ref
):
    block = mixed_ref.shape[0]
    width = mixed_ref.shape[1] // 2
    size = keep_ref.shape[0]
    upper = lax.broadcasted_iota(jnp.int32, (SLAB, block), 0) >= HD
    for group, first in slabs(width):
        tokens = (near_ref, far_ref, (an0_ref, an1_ref), (af0_ref, af1_ref), group, first, width)
        queries = queries_of(near_ref, far_ref, group, first, width).T
        keys = tokens_of(*tokens, 1)
        values = tokens_of(*tokens, 2).T
        outs = []
        for h in range(2):
            scores = dot_nn(keys, jnp.where(upper == (h == 1), queries, jnp.zeros_like(queries)))
            peak = jnp.max(scores, axis=0, keepdims=True)
            expo = jnp.exp2((scores - peak) * EXPO)
            weight = total(expo)
            out = dot_nn(values[h * HD : (h + 1) * HD], expo.astype(BF))
            outs.append(out * (1.0 / weight))
            head = (group * width + first) // HD + h
            log_ref[head : head + 1, :] = peak * EXPO + jnp.log2(weight)
        at = group * width + first
        mixed_ref[:, at : at + SLAB] = jnp.concatenate(outs, 0).T.astype(BF)
    for rows, out_ref in ((slice(size, 2 * size), send_ref), (slice(0, size), keep_ref)):
        branch = dot_nt(mixed_ref[rows, :width], own_w_ref[...])
        branch = branch + dot_nt(mixed_ref[rows, width:], other_w_ref[...])
        out_ref[...] = branch.astype(out_ref.dtype)


def middle_kernel(keep_ref, far_ref, bias_ref, rows_ref, mod_ref, branch_ref, middle_ref, second_ref):
    branch = keep_ref[...] + far_ref[...].astype(F32) + bias_ref[...]
    middle = rows_ref[...].astype(F32) + mod_ref[2:3] * branch
    unit, _ = unit_rows(middle)
    branch_ref[...] = branch.astype(BF)
    middle_ref[...] = middle
    second_ref[...] = (unit * (1.0 + mod_ref[4:5]) + mod_ref[3:4]).astype(BF)


def mlp_kernel(
    rows_ref, own_w1_ref, other_w1_ref, bias_ref, own_w2_ref, other_w2_ref, act_out, slope_out, out_ref, act_ref, slope_ref, sems
):
    width = own_w1_ref.shape[1]
    tile = 256
    copies = []
    for group, w1_ref in enumerate((own_w1_ref, other_w1_ref)):
        for first in range(0, width, tile):
            cols = slice(group * width + first, group * width + first + tile)
            value, slope = gelu_both(dot_nn(rows_ref[...], w1_ref[:, first : first + tile]) + bias_ref[:, cols])
            act_ref[:, cols] = value.astype(BF)
            slope_ref[:, cols] = slope.astype(BF)
        cols = slice(group * width, (group + 1) * width)
        for i, (ref, out) in enumerate(((act_ref, act_out), (slope_ref, slope_out))):
            copies.append(pltpu.make_async_copy(ref.at[:, cols], out.at[:, cols], sems.at[group, i]))
            copies[-1].start()
    feed = dot_nt(act_ref[:, :width], own_w2_ref[...]) + dot_nt(act_ref[:, width:], other_w2_ref[...])
    out_ref[...] = feed.astype(out_ref.dtype)
    for copy in copies:
        copy.wait()


def layer_end_kernel(keep_ref, far_ref, bias_ref, middle_ref, mod_ref, feed_ref, out_ref):
    feed = keep_ref[...] + far_ref[...].astype(F32) + bias_ref[...]
    feed_ref[...] = feed.astype(BF)
    out_ref[...] = (middle_ref[...] + mod_ref[5:6] * feed).astype(BF)


def grad_feed_kernel(grad_ref, feed_ref, mod_ref, out_ref, sums_ref):
    grad = grad_ref[...].astype(F32)
    out = (mod_ref[5:6] * grad).astype(BF)
    out_ref[...] = out
    sums_ref[0:1] = total(grad * feed_ref[...].astype(F32))
    sums_ref[1:2] = total(out.astype(F32))


def grad_mlp_kernel(
    rows_ref, own_w2_ref, other_w2_ref, slope_in, own_w1_ref, other_w1_ref, hidden_out, sums_ref, out_ref, hidden_ref, slope_ref, sems
):
    width = own_w2_ref.shape[1]
    tile = 256
    halves = [slice(group * width, (group + 1) * width) for group in range(2)]
    slopes = [
        pltpu.make_async_copy(slope_in.at[:, cols], slope_ref.at[:, cols], sems.at[0, group])
        for group, cols in enumerate(halves)
    ]
    hiddens = [
        pltpu.make_async_copy(hidden_ref.at[:, cols], hidden_out.at[:, cols], sems.at[1, group])
        for group, cols in enumerate(halves)
    ]
    for copy in slopes:
        copy.start()
    for group, w2_ref in enumerate((own_w2_ref, other_w2_ref)):
        for first in range(0, width, tile):
            cols = slice(group * width + first, group * width + first + tile)
            grad = dot_nn(rows_ref[...], w2_ref[:, first : first + tile])
            if first == 0:
                slopes[group].wait()
            grad = (grad * slope_ref[:, cols].astype(F32)).astype(BF)
            hidden_ref[:, cols] = grad
            sums_ref[:, cols] = total(grad.astype(F32))
        hiddens[group].start()
    second = dot_nt(hidden_ref[:, :width], own_w1_ref[...]) + dot_nt(hidden_ref[:, width:], other_w1_ref[...])
    out_ref[...] = second.astype(out_ref.dtype)
    for copy in hiddens:
        copy.wait()


def grad_middle_kernel(keep_ref, far_ref, middle_ref, branch_ref, grad_ref, mod_ref, out_ref, rows_ref, sums_ref):
    grad = keep_ref[...] + far_ref[...].astype(F32)
    unit, inverse = unit_rows(middle_ref[...])
    sums_ref[0:1] = total(grad)
    sums_ref[1:2] = total(grad * unit)
    grad = norm_back(unit, inverse, grad, mod_ref[4:5]) + grad_ref[...].astype(F32)
    out_ref[...] = grad
    sums_ref[2:3] = total(grad * branch_ref[...].astype(F32))
    rows = (mod_ref[2:3] * grad).astype(BF)
    rows_ref[...] = rows
    sums_ref[3:4] = total(rows.astype(F32))


def grad_attend_kernel(
    rows_near_ref,
    rows_far_ref,
    own_w_ref,
    other_w_ref,
    near_ref,
    far_ref,
    an0_ref,
    an1_ref,
    af0_ref,
    af1_ref,
    mixed_ref,
    log_ref,
    out_ref,
    keep_ref,
    send_ref,
    grad_ref,
):
    block = mixed_ref.shape[0]
    width = mixed_ref.shape[1] // 2
    size = rows_near_ref.shape[0]
    scale = HD ** (-0.5)
    for part, rows_ref in enumerate((rows_near_ref, rows_far_ref)):
        for group, w_ref in enumerate((own_w_ref, other_w_ref)):
            grad_ref[part * size : (part + 1) * size, group * width : (group + 1) * width] = dot_nn(
                rows_ref[...], w_ref[...]
            ).astype(BF)
    upper = lax.broadcasted_iota(jnp.int32, (SLAB, block), 0) >= HD
    right = lax.broadcasted_iota(jnp.int32, (block, SLAB), 1) >= HD
    for group, first in slabs(width):
        at = group * width + first
        tokens = (near_ref, far_ref, (an0_ref, an1_ref), (af0_ref, af1_ref), group, first, width)
        queries = queries_of(near_ref, far_ref, group, first, width)
        grad = grad_ref[:, at : at + SLAB]
        keys, values = tokens_of(*tokens, 1), tokens_of(*tokens, 2)
        queries_t, grad_t, keys_t = queries.T, grad.T, keys.T
        inner = grad_t.astype(F32) * mixed_ref[:, at : at + SLAB].T.astype(F32)
        none = jnp.zeros_like(queries_t)
        none_r = jnp.zeros_like(queries)
        outs, key_sum, value_sum = [], None, None
        for h in range(2):
            head = at // HD + h
            delta = total(inner[h * HD : (h + 1) * HD])
            scores = dot_nn(keys, jnp.where(upper == (h == 1), queries_t, none))
            probs = jnp.exp2(scores * EXPO - log_ref[head : head + 1, :])
            grad_w = dot_nn(values, jnp.where(upper == (h == 1), grad_t, none))
            grad_s = (probs * (grad_w - delta)).astype(BF)
            value_part = dot_nn(probs.astype(BF), jnp.where(right == (h == 1), grad, none_r))
            key_part = dot_nn(grad_s, jnp.where(right == (h == 1), queries, none_r))
            key_sum = key_part if h == 0 else key_sum + key_part
            value_sum = value_part if h == 0 else value_sum + value_part
            outs.append(dot_nn(keys_t[h * HD : (h + 1) * HD], grad_s))
        out_ref[:, at : at + SLAB] = (jnp.concatenate(outs, 0).T * scale).astype(BF)
        for which, term in enumerate((key_sum * scale, value_sum)):
            cols = group * 2 * width + which * width + first
            turned = (1 - group) * 2 * width + which * width + first
            keep_ref[:, cols : cols + SLAB] = term[:block]
            send_ref[:, turned : turned + SLAB] = term[block:].astype(BF)


def grad_normed_kernel(part, query_ref, keep_ref, got_ref, own_w_ref, other_w_ref, triple_ref, out_ref, sums_ref):
    size, width = triple_ref.shape[0], query_ref.shape[1] // 2
    rows = slice(part * size, (part + 1) * size)
    for group in range(2):
        at = group * 3 * width
        cols = slice(group * 2 * width, (group + 1) * 2 * width)
        triple_ref[:, at : at + width] = query_ref[rows, group * width : (group + 1) * width]
        triple_ref[:, at + width : at + 3 * width] = (
            keep_ref[rows, cols] + got_ref[rows, cols].astype(F32)
        ).astype(BF)
    out = dot_nt(triple_ref[:, : 3 * width], own_w_ref[...]) + dot_nt(triple_ref[:, 3 * width :], other_w_ref[...])
    out_ref[...] = out.astype(out_ref.dtype)
    sums_ref[...] = total(triple_ref[...].astype(F32))


def grad_rows_kernel(keep_ref, far_ref, rows_ref, middle_ref, mod_ref, out_ref, sums_ref):
    grad = keep_ref[...] + far_ref[...].astype(F32)
    unit, inverse = unit_rows(rows_ref[...].astype(F32))
    sums_ref[0:1] = total(grad)
    sums_ref[1:2] = total(grad * unit)
    out_ref[...] = (norm_back(unit, inverse, grad, mod_ref[1:2]) + middle_ref[...]).astype(BF)


CHUNKS = 4


def weight_kernel(lefts, rights, flag_ref, *refs):
    count = lefts + rights
    out_refs = refs[2 * count : -7]
    left_rows, left_all, right_all, keep_all, send_all, sems, out_sems = refs[-7:]

    for section in range(2):
        here = refs[section * count : (section + 1) * count]

        @pl.when(flag_ref[0] == section)
        def _():
            copies = []
            for some, to in ((here[:lefts], left_rows), (here[lefts:], right_all)):
                at = 0
                for ref in some:
                    rows = slice(at, at + ref.shape[0])
                    copies.append((pltpu.make_async_copy(ref, to.at[rows], sems.at[len(copies)]), rows))
                    copies[-1][0].start()
                    at += ref.shape[0]
            for copy, rows in copies[:lefts]:
                copy.wait()
                left_all[:, rows] = left_rows[rows].T
            for copy, _ in copies[lefts:]:
                copy.wait()

    rows, width = keep_all.shape
    tile = rows // CHUNKS
    copies = []
    for i in range(CHUNKS):
        part = slice(i * tile, (i + 1) * tile)
        keep_all[part] = dot_nn(left_all[part], right_all[:, :width]).astype(BF)
        send_all[part] = dot_nn(left_all[part], right_all[:, width:]).astype(BF)
        copies.append(pltpu.make_async_copy(keep_all.at[part], out_refs[0].at[part], out_sems.at[0, i]))
        copies.append(pltpu.make_async_copy(send_all.at[part], out_refs[i + 1], out_sems.at[1, i]))
        copies[-2].start()
        copies[-1].start()
    for copy in copies:
        copy.wait()


def weight_grad(first, second, section, token):
    lefts, rights = first
    tokens = sum(x.shape[0] for x in lefts)
    rows, cols = lefts[0].shape[1], rights[0].shape[1]
    ins = (*lefts, *rights, *second[0], *second[1])
    return call(
        functools.partial(weight_kernel, len(lefts), len(rights)),
        ins,
        [like(rows, cols // 2, BF)] + [like(rows // CHUNKS, cols // 2, BF)] * CHUNKS,
        scratch=[
            pltpu.VMEM((tokens, rows), BF),
            pltpu.VMEM((rows, tokens), BF),
            pltpu.VMEM((tokens, cols), BF),
            pltpu.VMEM((rows, cols // 2), BF),
            pltpu.VMEM((rows, cols // 2), BF),
            pltpu.SemaphoreType.DMA((len(lefts) + len(rights),)),
            pltpu.SemaphoreType.DMA((2, CHUNKS)),
        ],
        token=token,
        flag=section,
        far_in=range(len(ins)),
        far_out=range(1 + CHUNKS),
    )


def add_kernel(count, *refs):
    out_ref, one_all, two_all, sems = refs[-4:]
    size = out_ref.shape[0] // CHUNKS
    first, copies = 0, []
    for one_ref, *got in (refs[i * (1 + CHUNKS) : (i + 1) * (1 + CHUNKS)] for i in range(count)):
        cols = slice(first, first + one_ref.shape[1])
        first = cols.stop
        copies.append(pltpu.make_async_copy(one_ref, one_all.at[:, cols], sems.at[len(copies)]))
        for i, two_ref in enumerate(got):
            rows = slice(i * size, (i + 1) * size)
            copies.append(pltpu.make_async_copy(two_ref, two_all.at[rows, cols], sems.at[len(copies)]))
    for copy in copies:
        copy.start()
    for copy in copies:
        copy.wait()
    for i in range(CHUNKS):
        rows = slice(i * size, (i + 1) * size)
        out_ref[rows] = (one_all[rows].astype(F32) + two_all[rows].astype(F32)).astype(BF)


def copy_kernel(from_ref, out_ref):
    out_ref[...] = from_ref[...]


def tied(block, token):
    if token is None:
        return block
    token = token if isinstance(token, tuple) else (token,)
    return lax.optimization_barrier((block, *token))[0]


def forward_steps(rows, mod, weights):
    w_qkv, b_qkv, w_out, b_out, w_fc1, b_fc1, w_fc2 = weights
    size, width = rows.shape
    local = w_out[0].shape[1]
    hidden = w_fc1[0].shape[1]
    token = yield None, ()
    (normed,) = call(first_norm_kernel, (rows, mod), [like(size, width, BF)], token=token)
    normed_far = swap(normed, 2)
    triple_outs = [like(size, 6 * local, BF), like(size, 2 * local, BF), like(size, 2 * local, BF)]
    triple, *sends = call(triple_kernel, (normed, *w_qkv, b_qkv), triple_outs)
    away = [swap(send, 1) for send in sends]
    token = yield triple, ()
    normed_far = tied(normed_far, token)
    triple_far, *sends = call(triple_kernel, (normed_far, *w_qkv, b_qkv), triple_outs, token=token)
    tokens = (triple, triple_far, *away, *(swap(send, 1) for send in sends))
    mixed, log, keep, send = call(
        attend_kernel,
        (*tokens, *w_out),
        [
            like(2 * size, 2 * local, BF),
            like(2 * local // HD, 2 * size, F32),
            like(size, width, F32),
            like(size, width, BF),
        ],
        token=token,
    )
    far = swap(send, 2)
    token = yield keep, ()
    branch, middle, second = call(
        middle_kernel,
        (keep, tied(far, token), b_out[0:1], rows, mod),
        [like(size, width, BF), like(size, width, F32), like(size, width, BF)],
        token=token,
    )
    second_far = swap(second, 2)
    outs = [like(size, 2 * hidden, BF), like(size, 2 * hidden, BF)]
    scratch = [
        pltpu.VMEM((size, 2 * hidden), BF),
        pltpu.VMEM((size, 2 * hidden), BF),
        pltpu.SemaphoreType.DMA((2, 2)),
    ]
    act, slope, keep = call(
        mlp_kernel,
        (second, *w_fc1, b_fc1, *w_fc2),
        [*outs, like(size, width, F32)],
        scratch=scratch,
        far_out=(0, 1),
    )
    token = yield keep, ()
    second_far = tied(second_far, token)
    act_far, slope_far, send = call(
        mlp_kernel,
        (second_far, *w_fc1, b_fc1, *w_fc2),
        [*outs, like(size, width, BF)],
        scratch=scratch,
        token=token,
        far_out=(0, 1),
    )
    far = swap(send, 2)
    token = yield send, ()
    feed, result = call(
        layer_end_kernel,
        (keep, tied(far, token), b_out[1:2], middle, mod),
        [like(size, width, BF), like(size, width, BF)],
        token=token,
    )
    state = (
        rows, (normed, normed_far), tokens, mixed, log, branch, middle,
        (second, second_far), (act, act_far), (slope, slope_far), feed,
    )
    return result, state


def backward_steps(grad, mod, weights, state, flops=0):
    w_qkv, b_qkv, w_out, b_out, w_fc1, b_fc1, w_fc2 = weights
    rows, normed, tokens, mixed, log, branch, middle, second, acts, slopes, feed = state
    size, width = rows.shape
    local = w_out[0].shape[1]
    hidden = w_fc1[0].shape[1]
    token = yield None, ()
    feed_rows, sums_feed = call(
        grad_feed_kernel, (grad, feed, mod), [like(size, width, BF), like(2, width, F32)], token=token
    )
    feed_far = swap(feed_rows, 2)
    outs = [like(size, 2 * hidden, BF), like(1, 2 * hidden, F32)]
    scratch = [
        pltpu.VMEM((size, 2 * hidden), BF),
        pltpu.VMEM((size, 2 * hidden), BF),
        pltpu.SemaphoreType.DMA((2, 2)),
    ]
    hidden_near, sums_near, keep = call(
        grad_mlp_kernel,
        (feed_rows, *w_fc2, slopes[0], *w_fc1),
        [*outs, like(size, width, F32)],
        scratch=scratch,
        far_in=(3,),
        far_out=(0,),
    )
    token = yield keep, ()
    feed_far = tied(feed_far, token)
    hidden_far, sums_far, send = call(
        grad_mlp_kernel,
        (feed_far, *w_fc2, slopes[1], *w_fc1),
        [*outs, like(size, width, BF)],
        scratch=scratch,
        token=token,
        far_in=(3,),
        far_out=(0,),
    )
    far = swap(send, 2)
    token = yield send, ((3, (feed_rows, feed_far), acts),)
    grad_middle, branch_rows, sums_middle = call(
        grad_middle_kernel,
        (keep, tied(far, token), middle, branch, grad, mod),
        [like(size, width, F32), like(size, width, BF), like(4, width, F32)],
        token=token,
    )
    branch_far = swap(branch_rows, 2)
    token = yield branch_rows, ((2, second, (hidden_near, hidden_far)),)
    branch_far = tied(branch_far, token)
    queries, kept, send = call(
        grad_attend_kernel,
        (branch_rows, branch_far, *w_out, *tokens, mixed, log),
        [
            like(2 * size, 2 * local, BF),
            like(2 * size, 4 * local, F32),
            like(2 * size, 4 * local, BF),
        ],
        scratch=[pltpu.VMEM((2 * size, 2 * local), BF)],
        token=token,
        flops=flops,
    )
    got = swap(send, 1)
    token = yield kept, ((1, (branch_rows, branch_far), (mixed,)),)
    outs = [like(size, 6 * local, BF), like(size, width, BF), like(1, 6 * local, F32)]
    triple_far, send, sums_triple_far = call(
        functools.partial(grad_normed_kernel, 1), (queries, kept, got, *w_qkv), outs, token=token
    )
    far = swap(send, 2)
    outs[1] = like(size, width, F32)
    triple_near, keep, sums_triple = call(
        functools.partial(grad_normed_kernel, 0), (queries, kept, got, *w_qkv), outs, token=send
    )
    token = yield keep, ((0, normed, (triple_near, triple_far)),)
    grad_rows, sums_rows = call(
        grad_rows_kernel,
        (keep, tied(far, token), rows, grad_middle, mod),
        [like(size, width, BF), like(2, width, F32)],
        token=token,
    )
    return grad_rows, (sums_rows, sums_middle, sums_feed, sums_triple, sums_triple_far, sums_near, sums_far)


def small_sums(raw):
    sums_rows, sums_middle, sums_feed, sums_triple, sums_triple_far, sums_near, sums_far = raw
    grad_mod = jnp.concatenate(
        [sums_rows, sums_middle[2:3], sums_middle[0:2], sums_feed[0:1]], 0
    ).reshape(1, -1)
    return grad_mod, (
        (sums_triple + sums_triple_far)[0],
        (sums_near + sums_far)[0],
        jnp.concatenate([sums_middle[3:4], sums_feed[1:2]], 0),
    )


def chain_steps(ends, mod, weights, flops):
    sent, state_one = yield from forward_steps(ends, mod, weights)
    arrived = lax.ppermute(sent, "section", [(0, 1)])
    yield sent, ()
    out, state_two = yield from forward_steps(arrived, mod, weights)
    yield out, ()
    back_two = yield from backward_steps(ends, mod, weights, state_two)
    arrived = lax.ppermute(back_two[0], "section", [(1, 0)])
    yield back_two[0], ()
    back_one = yield from backward_steps(arrived, mod, weights, state_one, flops)
    yield back_one[0], ()
    return out, back_two, back_one


def side_by_side(chains, section):
    results = [None] * len(chains)
    products, sums, pending, begun = {}, {}, [], [None, None]
    after = {0: 2}
    for chain in chains:
        next(chain)
    token = None
    while pending or any(result is None for result in results):
        ready = {}
        if any(which == 0 for which, _, _ in pending):
            token = (token, sums[3])
        for i, chain in enumerate(chains):
            try:
                token, made = chain.send(token)
            except StopIteration as stop:
                results[i] = stop.value
                continue
            for which, lefts, rights in made:
                both = ready.setdefault(which, ([], []))
                both[0].extend(lefts)
                both[1].extend(rights)
        for which, keep, got in pending:
            parts = (keep, *got)
            if which == 1:
                waiting = parts
                continue
            if which in after:
                token = (token, sums[after[which]])
                parts = (*parts, *waiting)
            rows, cols = keep.shape[0], sum(x.shape[1] for x in parts[:: 1 + CHUNKS])
            count = len(parts) // (1 + CHUNKS)
            (token,) = call(
                functools.partial(add_kernel, count),
                parts,
                [like(rows, cols, BF)],
                scratch=[
                    pltpu.VMEM((rows, cols), BF),
                    pltpu.VMEM((rows, cols), BF),
                    pltpu.SemaphoreType.DMA((len(parts),)),
                ],
                token=token,
                far_in=range(len(parts)),
            )
            if which in after and lax.axis_size("dp") <= 4:
                sums[which], begun = line_reduce(token)
            else:
                sums[which] = lax.psum_scatter(token, "dp", scatter_dimension=0, tiled=True)
        pending = []
        for which, operands in ready.items():
            if which not in products:
                products[which] = operands
                continue
            keep, *sends = weight_grad(operands, products[which], section, token)
            token = keep
            pending.append((which, keep, [swap(send, 1) for send in sends]))
    return results, sums, token, begun


def body(
    boundary,
    conditioning,
    query_key_value_weight,
    query_value_bias,
    attention_output_weight,
    output_biases,
    first_mlp_weight,
    first_mlp_bias,
    second_mlp_weight,
    w_ada,
    ada_bias,
):
    leading = lax.axis_index("section") == 0
    ends = boundary[0]
    width, _, local = query_key_value_weight.shape[1:]
    tensor_no = lax.axis_index("tensor")
    dp_no = lax.axis_index("dp")
    tensor_count = lax.axis_size("tensor")
    dp_count = lax.axis_size("dp")
    w_qkv = jnp.concatenate([query_key_value_weight[0, :, i] for i in range(3)], 1)
    qv = query_value_bias[0].astype(F32)
    b_qkv = jnp.concatenate([qv[0], jnp.zeros_like(qv[0]), qv[1]])[None]
    w_out, w_fc1, w_fc2 = attention_output_weight[0], first_mlp_weight[0], second_mlp_weight[0]
    hidden = w_fc1.shape[1]
    vectors = jnp.concatenate([b_qkv, first_mlp_bias.astype(F32)], 1)
    other = swap(vectors, 1)
    weights = (
        (w_qkv, swap(w_qkv, 1)),
        jnp.concatenate([b_qkv, other[:, : 3 * local]], 1),
        (w_out, swap(w_out, 1)),
        output_biases[0].astype(F32),
        (w_fc1, swap(w_fc1, 1)),
        jnp.concatenate([vectors[:, 3 * local :], other[:, 3 * local :]], 1),
        (w_fc2, swap(w_fc2, 1)),
    )
    ada_weight = w_ada[0]
    cond_vals = conditioning.astype(F32)
    cond_act = jax.nn.silu(cond_vals).astype(BF)
    mods = (dot_nn(cond_act, ada_weight) + ada_bias[0].astype(F32)).reshape(2, 6, width)

    section = lax.axis_index("section").astype(jnp.int32).reshape(1)
    chains, sums, token, begun = side_by_side(
        [chain_steps(ends[b], mods[b], weights, b * 10**11) for b in range(ends.shape[0])], section
    )
    outs = [chain[0] for chain in chains]
    raw = [(chain[1][1], chain[2][1]) for chain in chains]
    leaves, kind = jax.tree.flatten(raw)
    raw = jax.tree.unflatten(kind, lax.optimization_barrier((*leaves, token))[:-1])
    backs_two = [(chain[1][0], *small_sums(two)) for chain, (two, _) in zip(chains, raw)]
    backs_one = [(chain[2][0], *small_sums(one)) for chain, (_, one) in zip(chains, raw)]

    g_both, g_fc1, g_fc2 = (sums[i].astype(F32) for i in (0, 2, 3))
    g_qkv, g_proj = g_both[:, : 3 * local], g_both[:, 3 * local :]
    g_qkv = jnp.stack([g_qkv[:, i * local : (i + 1) * local] for i in range(3)], 1)

    pick = lambda one, two: jnp.where(leading, one, two)
    grad_mods = jnp.concatenate(
        [pick(one[1], two[1]) for one, two in zip(backs_one, backs_two)], 0
    )
    owned_triple, owned_hidden, partial = (
        pick(
            backs_one[0][2][i] + backs_one[1][2][i],
            backs_two[0][2][i] + backs_two[1][2][i],
        )
        for i in range(3)
    )
    def placed(vector):
        size = vector.shape[0] // 2
        full = jnp.zeros((tensor_count * size,), F32)
        for part, where in ((vector[:size], tensor_no), (vector[size:], tensor_no ^ 1)):
            full = lax.dynamic_update_slice(full, part, (where * size,))
        return full

    span = 3 * local
    queries = jnp.concatenate([owned_triple[:local], owned_triple[span : span + local]])
    values = jnp.concatenate([owned_triple[2 * local : span], owned_triple[span + 2 * local :]])
    flat = jnp.concatenate(
        [
            grad_mods.reshape(-1),
            placed(queries),
            placed(values),
            placed(owned_hidden),
            partial.reshape(-1),
        ]
    )
    (flat,) = call(
        copy_kernel, (flat.reshape(-1, width),), [like(flat.size // width, width, F32)], token=token, flops=10**11
    )
    flat = tied(tensor_sum(flat), begun[0]).reshape(-1)
    grad_mods = flat[: 12 * width].reshape(2, 6 * width)
    biases = flat[12 * width :]
    everything = over_dp(
        jnp.concatenate([grad_mods.reshape(-1), biases, cond_act.astype(F32).reshape(-1)])[None]
    )
    mods_end = 12 * width
    all_mods = everything[:, :mods_end].reshape(2 * dp_count, 6 * width)
    all_acts = everything[:, -2 * width :].reshape(2 * dp_count, width)
    biases = jnp.sum(everything[:, mods_end : -2 * width], axis=0)
    place = dp_no * tensor_count + tensor_no
    shares = dp_count * tensor_count

    def own_share(vector):
        size = vector.shape[0] // shares
        return lax.dynamic_slice(vector, (place * size,), (size,))[None]

    hidden_all = biases.shape[0] - 4 * width
    g_qv_bias = own_share(biases[: 2 * width])
    g_fc1_bias = own_share(biases[2 * width : 2 * width + hidden_all])
    g_out_bias = own_share(biases[2 * width + hidden_all :])
    g_ada_bias = own_share(jnp.sum(all_mods, axis=0))
    share = width // shares
    act_share = lax.dynamic_slice(all_acts, (0, place * share), (all_acts.shape[0], share))
    g_ada = lax.dot_general(
        act_share, all_mods, (((0,), (0,)), ((), ())), precision=precise, preferred_element_type=F32
    )

    cut = 6 * width // tensor_count
    mods_cut = lax.dynamic_slice(grad_mods, (0, tensor_no * cut), (2, cut))
    ada_cut = lax.dynamic_slice(ada_weight, (0, tensor_no * cut), (width, cut))
    back_cond = lax.dot_general(
        mods_cut,
        ada_cut.astype(F32),
        (((1,), (1,)), ((), ())),
        precision=precise,
        preferred_element_type=F32,
    )
    back_cond = tied(back_cond, (everything, *(begun[1] or ())))
    back_cond = back_cond + lax.ppermute(back_cond, "section", [(0, 1), (1, 0)])
    cond_total = tensor_sum(back_cond)
    sig = jax.nn.sigmoid(cond_vals)
    cond_grad = cond_total * sig * (1.0 + cond_vals * (1.0 - sig))

    rows_out = jnp.stack([pick(back[0], out) for back, out in zip(backs_one, outs)])[None]
    return (
        rows_out,
        cond_grad,
        g_qkv[None],
        g_qv_bias,
        g_proj[None],
        g_out_bias,
        g_fc1[None],
        g_fc1_bias,
        g_fc2[None],
        g_ada[None],
        g_ada_bias,
    )


def solution(mesh):
    in_specs = (
        P("section", "dp", "tensor", None),
        P("dp", None),
        P("section", None, None, "tensor"),
        P("section", None, "tensor"),
        P("section", None, "tensor"),
        P("section", None, None),
        P("section", None, "tensor"),
        P("section", "tensor"),
        P("section", None, "tensor"),
        P("section", None, None),
        P("section", None),
    )
    out_specs = (
        P("section", "dp", "tensor", None),
        P("dp", None),
        P("section", "dp", None, "tensor"),
        P("section", ("dp", "tensor")),
        P("section", "dp", "tensor"),
        P("section", ("dp", "tensor")),
        P("section", "dp", "tensor"),
        P("section", ("dp", "tensor")),
        P("section", "dp", "tensor"),
        P("section", ("dp", "tensor"), None),
        P("section", ("dp", "tensor")),
    )
    return jax.shard_map(body, mesh=mesh, in_specs=in_specs, out_specs=out_specs, check_vma=False)
```

```python
import functools

import jax
import jax.numpy as jnp
from jax import lax
from jax.experimental import pallas as pl
from jax.experimental.pallas import tpu as pltpu
from jax.sharding import PartitionSpec as P

HD = 64
SLAB = 2 * HD
EXPO = HD ** (-0.5) * 1.4426950408889634
BF = jnp.bfloat16
F32 = jnp.float32
precise = lax.Precision.HIGHEST


def swap(block, bit):
    count = lax.axis_size("tensor")
    return lax.ppermute(block, "tensor", [(i, i ^ bit) for i in range(count)])


def tensor_sum(block):
    count = lax.axis_size("tensor")
    bit = 1
    while bit < count:
        block = block + swap(block, bit)
        bit *= 2
    return block


TIMES = {
    "first_norm_kernel": 1,
    "triple_kernel": 3,
    "attend_kernel": 8,
    "middle_kernel": 1,
    "mlp_kernel": 6,
    "layer_end_kernel": 1,
    "grad_feed_kernel": 1,
    "grad_mlp_kernel": 6,
    "grad_middle_kernel": 2,
    "grad_attend_kernel": 11,
    "grad_normed_kernel": 3,
    "grad_rows_kernel": 1,
    "weight_kernel": 6,
    "add_kernel": 1,
    "copy_kernel": 1,
}
SHARE = 1


def over_dp(block, begun):
    count = lax.axis_size("dp")
    if count & (count - 1):
        return lax.all_gather(block, "dp", axis=0, tiled=True)
    bit = 1
    while bit < count:
        block = tied(block, begun.pop(0) if begun else None)
        other = lax.ppermute(block, "dp", [(i, i ^ bit) for i in range(count)])
        block = jnp.concatenate([block, other], 0)
        bit *= 2
    return block


def line_reduce(block):
    count, place = lax.axis_size("dp"), lax.axis_index("dp")
    size = block.shape[0] // count

    def chunk(owner):
        at = jnp.clip(owner, 0, count - 1) * size
        return lax.dynamic_slice(block, (at, 0), (size, block.shape[1])).astype(F32)

    came = []
    up = down = jnp.zeros((size, block.shape[1]), BF)
    for step in range(1, count):
        up = (chunk(place + count - step) + up.astype(F32)).astype(BF)
        down = (chunk(place - count + step) + down.astype(F32)).astype(BF)
        up, down = lax.optimization_barrier((up, down))
        up = lax.ppermute(up, "dp", [(i, i + 1) for i in range(step)])
        down = lax.ppermute(down, "dp", [(i, i - 1) for i in range(count - step, count)])
        came.append((up, down))
    return chunk(place) + up.astype(F32) + down.astype(F32), came


def call(kernel, ins, outs, scratch=(), token=None, flag=None, flops=0, far_in=(), far_out=()):
    name = getattr(kernel, "func", kernel).__name__
    vmem = pl.BlockSpec(memory_space=pltpu.VMEM)
    anywhere = pl.BlockSpec(memory_space=pl.ANY)
    specs = [anywhere if i in far_in else vmem for i in range(len(ins))]
    if flag is not None:
        ins = (flag, *ins)
        specs = [pl.BlockSpec(memory_space=pltpu.SMEM), *specs]
    body = kernel
    if token is not None:
        token = token if isinstance(token, tuple) else (token,)
        place = len(ins)
        ins = (*ins, *token)
        specs += [anywhere] * len(token)

        def body(*refs):
            kernel(*refs[:place], *refs[len(ins) :])

    shift = 0 if flag is None else 1
    ins = [outside(x) if i - shift in far_in else x for i, x in enumerate(ins)]
    results = pl.pallas_call(
        body,
        in_specs=specs,
        out_specs=[anywhere if i in far_out else vmem for i in range(len(outs))],
        out_shape=list(outs),
        scratch_shapes=list(scratch),
        compiler_params=pltpu.CompilerParams(vmem_limit_bytes=(20 if name == "weight_kernel" else 14) << 20),
        cost_estimate=pl.CostEstimate(flops=flops or int(TIMES[name] * SHARE * 1.15e9), bytes_accessed=0, transcendentals=0),
    )(*ins)
    return [outside(x) if i in far_out else x for i, x in enumerate(results)]


def outside(block):
    return pltpu.with_memory_space_constraint(block, pltpu.HBM)


def like(rows, cols, kind):
    return jax.ShapeDtypeStruct((rows, cols), kind)


def dot_nn(left, right):
    return jnp.dot(left, right, preferred_element_type=F32)


def dot_nt(left, right):
    return lax.dot_general(left, right, (((1,), (1,)), ((), ())), preferred_element_type=F32)


def unit_rows(rows):
    center = rows - jnp.mean(rows, axis=-1, keepdims=True)
    spread = jnp.mean(center * center, axis=-1, keepdims=True)
    inverse = lax.rsqrt(spread + 1e-06)
    return center * inverse, inverse


def norm_back(unit, inverse, grad, factor):
    grad_unit = grad * (1.0 + factor)
    return inverse * (
        grad_unit
        - jnp.mean(grad_unit, axis=-1, keepdims=True)
        - unit * jnp.mean(grad_unit * unit, axis=-1, keepdims=True)
    )


def gelu_both(u):
    root = 0.7978845608028654
    square = u * u
    inner = root * (1.0 + 0.044715 * square)
    tanh = jnp.tanh(u * inner)
    half = 0.5 * (1.0 + tanh)
    slope = half + (0.5 * u) * (1.0 - tanh * tanh) * (root + (3.0 * 0.044715 * root) * square)
    return u * half, slope


def total(ref):
    return jnp.sum(ref, axis=0, keepdims=True)


def first_norm_kernel(rows_ref, mod_ref, out_ref):
    unit, _ = unit_rows(rows_ref[...].astype(F32))
    out_ref[...] = (unit * (1.0 + mod_ref[1:2]) + mod_ref[0:1]).astype(BF)


def triple_kernel(rows_ref, own_w_ref, other_w_ref, bias_ref, triple_ref, *send_refs):
    width = own_w_ref.shape[1]
    third = width // 3
    for group, w_ref in enumerate((own_w_ref, other_w_ref)):
        cols = slice(group * width, (group + 1) * width)
        part = (dot_nn(rows_ref[...], w_ref[...]) + bias_ref[:, cols]).astype(BF)
        triple_ref[:, cols] = part
        send_refs[1 - group][...] = part[:, third:]


def slabs(width):
    return [(group, first) for group in range(2) for first in range(0, width, SLAB)]


def tokens_of(near_ref, far_ref, away_near_ref, away_far_ref, group, first, width, which):
    here = group * 3 * width + which * width + first
    away = (which - 1) * width + first
    return jnp.concatenate(
        [ref[:, here : here + SLAB] for ref in (near_ref, far_ref)]
        + [refs[group][:, away : away + SLAB] for refs in (away_near_ref, away_far_ref)],
        0,
    )


def queries_of(near_ref, far_ref, group, first, width):
    start = group * 3 * width + first
    return jnp.concatenate([ref[:, start : start + SLAB] for ref in (near_ref, far_ref)], 0)


def attend_kernel(
    near_ref, far_ref, an0_ref, an1_ref, af0_ref, af1_ref, own_w_ref, other_w_ref, mixed_ref, log_ref, keep_ref, send_ref
):
    block = mixed_ref.shape[0]
    width = mixed_ref.shape[1] // 2
    size = keep_ref.shape[0]
    upper = lax.broadcasted_iota(jnp.int32, (SLAB, block), 0) >= HD
    for group, first in slabs(width):
        tokens = (near_ref, far_ref, (an0_ref, an1_ref), (af0_ref, af1_ref), group, first, width)
        queries = queries_of(near_ref, far_ref, group, first, width).T
        keys = tokens_of(*tokens, 1)
        values = tokens_of(*tokens, 2).T
        outs = []
        for h in range(2):
            scores = dot_nn(keys, jnp.where(upper == (h == 1), queries, jnp.zeros_like(queries)))
            peak = jnp.max(scores, axis=0, keepdims=True)
            expo = jnp.exp2((scores - peak) * EXPO)
            weight = total(expo)
            out = dot_nn(values[h * HD : (h + 1) * HD], expo.astype(BF))
            outs.append(out * (1.0 / weight))
            head = (group * width + first) // HD + h
            log_ref[head : head + 1, :] = peak * EXPO + jnp.log2(weight)
        at = group * width + first
        mixed_ref[:, at : at + SLAB] = jnp.concatenate(outs, 0).T.astype(BF)
    for rows, out_ref in ((slice(size, 2 * size), send_ref), (slice(0, size), keep_ref)):
        branch = dot_nt(mixed_ref[rows, :width], own_w_ref[...])
        branch = branch + dot_nt(mixed_ref[rows, width:], other_w_ref[...])
        out_ref[...] = branch.astype(out_ref.dtype)


def middle_kernel(keep_ref, far_ref, bias_ref, rows_ref, mod_ref, branch_ref, middle_ref, second_ref):
    branch = keep_ref[...] + far_ref[...].astype(F32) + bias_ref[...]
    middle = rows_ref[...].astype(F32) + mod_ref[2:3] * branch
    unit, _ = unit_rows(middle)
    branch_ref[...] = branch.astype(BF)
    middle_ref[...] = middle
    second_ref[...] = (unit * (1.0 + mod_ref[4:5]) + mod_ref[3:4]).astype(BF)


def mlp_kernel(
    rows_ref, own_w1_ref, other_w1_ref, bias_ref, own_w2_ref, other_w2_ref, act_out, slope_out, out_ref, act_ref
):
    width = own_w1_ref.shape[1]
    tile = 256
    for group, w1_ref in enumerate((own_w1_ref, other_w1_ref)):
        for first in range(0, width, tile):
            cols = slice(group * width + first, group * width + first + tile)
            value, slope = gelu_both(dot_nn(rows_ref[...], w1_ref[:, first : first + tile]) + bias_ref[:, cols])
            act_ref[:, cols] = value.astype(BF)
            act_out[:, cols] = value.astype(BF)
            slope_out[:, cols] = slope.astype(BF)
    feed = dot_nt(act_ref[:, :width], own_w2_ref[...]) + dot_nt(act_ref[:, width:], other_w2_ref[...])
    out_ref[...] = feed.astype(out_ref.dtype)


def layer_end_kernel(keep_ref, far_ref, bias_ref, middle_ref, mod_ref, feed_ref, out_ref):
    feed = keep_ref[...] + far_ref[...].astype(F32) + bias_ref[...]
    feed_ref[...] = feed.astype(BF)
    out_ref[...] = (middle_ref[...] + mod_ref[5:6] * feed).astype(BF)


def grad_feed_kernel(grad_ref, feed_ref, mod_ref, out_ref, sums_ref):
    grad = grad_ref[...].astype(F32)
    out = (mod_ref[5:6] * grad).astype(BF)
    out_ref[...] = out
    sums_ref[0:1] = total(grad * feed_ref[...].astype(F32))
    sums_ref[1:2] = total(out.astype(F32))


def grad_mlp_kernel(
    rows_ref, own_w2_ref, other_w2_ref, slope_in, own_w1_ref, other_w1_ref, hidden_out, sums_ref, out_ref, hidden_ref, slope_ref, sems
):
    width = own_w2_ref.shape[1]
    tile = 256
    halves = [slice(group * width, (group + 1) * width) for group in range(2)]
    slopes = [
        pltpu.make_async_copy(slope_in.at[:, cols], slope_ref.at[:, cols], sems.at[0, group])
        for group, cols in enumerate(halves)
    ]
    hiddens = [
        pltpu.make_async_copy(hidden_ref.at[:, cols], hidden_out.at[:, cols], sems.at[1, group])
        for group, cols in enumerate(halves)
    ]
    for copy in slopes:
        copy.start()
    for group, w2_ref in enumerate((own_w2_ref, other_w2_ref)):
        for first in range(0, width, tile):
            cols = slice(group * width + first, group * width + first + tile)
            grad = dot_nn(rows_ref[...], w2_ref[:, first : first + tile])
            if first == 0:
                slopes[group].wait()
            grad = (grad * slope_ref[:, cols].astype(F32)).astype(BF)
            hidden_ref[:, cols] = grad
            sums_ref[:, cols] = total(grad.astype(F32))
        hiddens[group].start()
    second = dot_nt(hidden_ref[:, :width], own_w1_ref[...]) + dot_nt(hidden_ref[:, width:], other_w1_ref[...])
    out_ref[...] = second.astype(out_ref.dtype)
    for copy in hiddens:
        copy.wait()


def grad_middle_kernel(keep_ref, far_ref, middle_ref, branch_ref, grad_ref, mod_ref, out_ref, rows_ref, sums_ref):
    grad = keep_ref[...] + far_ref[...].astype(F32)
    unit, inverse = unit_rows(middle_ref[...])
    sums_ref[0:1] = total(grad)
    sums_ref[1:2] = total(grad * unit)
    grad = norm_back(unit, inverse, grad, mod_ref[4:5]) + grad_ref[...].astype(F32)
    out_ref[...] = grad
    sums_ref[2:3] = total(grad * branch_ref[...].astype(F32))
    rows = (mod_ref[2:3] * grad).astype(BF)
    rows_ref[...] = rows
    sums_ref[3:4] = total(rows.astype(F32))


def grad_attend_kernel(
    rows_near_ref,
    rows_far_ref,
    own_w_ref,
    other_w_ref,
    near_ref,
    far_ref,
    an0_ref,
    an1_ref,
    af0_ref,
    af1_ref,
    mixed_ref,
    log_ref,
    out_ref,
    keep_ref,
    send_ref,
    grad_ref,
):
    block = mixed_ref.shape[0]
    width = mixed_ref.shape[1] // 2
    size = rows_near_ref.shape[0]
    scale = HD ** (-0.5)
    for part, rows_ref in enumerate((rows_near_ref, rows_far_ref)):
        for group, w_ref in enumerate((own_w_ref, other_w_ref)):
            grad_ref[part * size : (part + 1) * size, group * width : (group + 1) * width] = dot_nn(
                rows_ref[...], w_ref[...]
            ).astype(BF)
    upper = lax.broadcasted_iota(jnp.int32, (SLAB, block), 0) >= HD
    right = lax.broadcasted_iota(jnp.int32, (block, SLAB), 1) >= HD
    for group, first in slabs(width):
        at = group * width + first
        tokens = (near_ref, far_ref, (an0_ref, an1_ref), (af0_ref, af1_ref), group, first, width)
        queries = queries_of(near_ref, far_ref, group, first, width)
        grad = grad_ref[:, at : at + SLAB]
        keys, values = tokens_of(*tokens, 1), tokens_of(*tokens, 2)
        queries_t, grad_t, keys_t = queries.T, grad.T, keys.T
        inner = grad_t.astype(F32) * mixed_ref[:, at : at + SLAB].T.astype(F32)
        none = jnp.zeros_like(queries_t)
        none_r = jnp.zeros_like(queries)
        outs, key_sum, value_sum = [], None, None
        for h in range(2):
            head = at // HD + h
            delta = total(inner[h * HD : (h + 1) * HD])
            scores = dot_nn(keys, jnp.where(upper == (h == 1), queries_t, none))
            probs = jnp.exp2(scores * EXPO - log_ref[head : head + 1, :])
            grad_w = dot_nn(values, jnp.where(upper == (h == 1), grad_t, none))
            grad_s = (probs * (grad_w - delta)).astype(BF)
            value_part = dot_nn(probs.astype(BF), jnp.where(right == (h == 1), grad, none_r))
            key_part = dot_nn(grad_s, jnp.where(right == (h == 1), queries, none_r))
            key_sum = key_part if h == 0 else key_sum + key_part
            value_sum = value_part if h == 0 else value_sum + value_part
            outs.append(dot_nn(keys_t[h * HD : (h + 1) * HD], grad_s))
        out_ref[:, at : at + SLAB] = (jnp.concatenate(outs, 0).T * scale).astype(BF)
        for which, term in enumerate((key_sum * scale, value_sum)):
            cols = group * 2 * width + which * width + first
            turned = (1 - group) * 2 * width + which * width + first
            keep_ref[:, cols : cols + SLAB] = term[:block]
            send_ref[:, turned : turned + SLAB] = term[block:].astype(BF)


def grad_normed_kernel(part, query_ref, keep_ref, got_ref, own_w_ref, other_w_ref, triple_ref, out_ref, sums_ref):
    size, width = triple_ref.shape[0], query_ref.shape[1] // 2
    rows = slice(part * size, (part + 1) * size)
    for group in range(2):
        at = group * 3 * width
        cols = slice(group * 2 * width, (group + 1) * 2 * width)
        triple_ref[:, at : at + width] = query_ref[rows, group * width : (group + 1) * width]
        triple_ref[:, at + width : at + 3 * width] = (
            keep_ref[rows, cols] + got_ref[rows, cols].astype(F32)
        ).astype(BF)
    out = dot_nt(triple_ref[:, : 3 * width], own_w_ref[...]) + dot_nt(triple_ref[:, 3 * width :], other_w_ref[...])
    out_ref[...] = out.astype(out_ref.dtype)
    sums_ref[...] = total(triple_ref[...].astype(F32))


def grad_rows_kernel(keep_ref, far_ref, rows_ref, middle_ref, mod_ref, out_ref, sums_ref):
    grad = keep_ref[...] + far_ref[...].astype(F32)
    unit, inverse = unit_rows(rows_ref[...].astype(F32))
    sums_ref[0:1] = total(grad)
    sums_ref[1:2] = total(grad * unit)
    out_ref[...] = (norm_back(unit, inverse, grad, mod_ref[1:2]) + middle_ref[...]).astype(BF)


CHUNKS = 4


def weight_kernel(lefts, rights, flag_ref, *refs):
    count = lefts + rights
    out_refs = refs[2 * count : -7]
    left_rows, left_all, right_all, keep_all, send_all, sems, out_sems = refs[-7:]

    for section in range(2):
        here = refs[section * count : (section + 1) * count]

        @pl.when(flag_ref[0] == section)
        def _():
            copies = []
            for some, to in ((here[:lefts], left_rows), (here[lefts:], right_all)):
                at = 0
                for ref in some:
                    rows = slice(at, at + ref.shape[0])
                    copies.append((pltpu.make_async_copy(ref, to.at[rows], sems.at[len(copies)]), rows))
                    copies[-1][0].start()
                    at += ref.shape[0]
            for copy, rows in copies[:lefts]:
                copy.wait()
                left_all[:, rows] = left_rows[rows].T
            for copy, _ in copies[lefts:]:
                copy.wait()

    rows, width = keep_all.shape
    tile = rows // CHUNKS
    copies = []
    for i in range(CHUNKS):
        part = slice(i * tile, (i + 1) * tile)
        keep_all[part] = dot_nn(left_all[part], right_all[:, :width]).astype(BF)
        send_all[part] = dot_nn(left_all[part], right_all[:, width:]).astype(BF)
        copies.append(pltpu.make_async_copy(keep_all.at[part], out_refs[0].at[part], out_sems.at[0, i]))
        copies.append(pltpu.make_async_copy(send_all.at[part], out_refs[i + 1], out_sems.at[1, i]))
        copies[-2].start()
        copies[-1].start()
    for copy in copies:
        copy.wait()


def weight_grad(first, second, section, token):
    lefts, rights = first
    tokens = sum(x.shape[0] for x in lefts)
    rows, cols = lefts[0].shape[1], rights[0].shape[1]
    ins = (*lefts, *rights, *second[0], *second[1])
    return call(
        functools.partial(weight_kernel, len(lefts), len(rights)),
        ins,
        [like(rows, cols // 2, BF)] + [like(rows // CHUNKS, cols // 2, BF)] * CHUNKS,
        scratch=[
            pltpu.VMEM((tokens, rows), BF),
            pltpu.VMEM((rows, tokens), BF),
            pltpu.VMEM((tokens, cols), BF),
            pltpu.VMEM((rows, cols // 2), BF),
            pltpu.VMEM((rows, cols // 2), BF),
            pltpu.SemaphoreType.DMA((len(lefts) + len(rights),)),
            pltpu.SemaphoreType.DMA((2, CHUNKS)),
        ],
        token=token,
        flag=section,
        far_in=range(len(ins)),
        far_out=range(1 + CHUNKS),
    )


def add_kernel(count, *refs):
    out_ref, one_all, two_all, sems = refs[-4:]
    size = out_ref.shape[0] // CHUNKS
    first, copies = 0, []
    for one_ref, *got in (refs[i * (1 + CHUNKS) : (i + 1) * (1 + CHUNKS)] for i in range(count)):
        cols = slice(first, first + one_ref.shape[1])
        first = cols.stop
        for i, two_ref in enumerate(got):
            rows = slice(i * size, (i + 1) * size)
            for ref, to in ((one_ref.at[rows], one_all), (two_ref, two_all)):
                copies.append((i, pltpu.make_async_copy(ref, to.at[rows, cols], sems.at[len(copies)])))
    copies.sort(key=lambda pair: pair[0])
    for _, copy in copies:
        copy.start()
    for i in range(CHUNKS):
        for where, copy in copies:
            if where == i:
                copy.wait()
        rows = slice(i * size, (i + 1) * size)
        out_ref[rows] = (one_all[rows].astype(F32) + two_all[rows].astype(F32)).astype(BF)


def copy_kernel(from_ref, out_ref):
    out_ref[...] = from_ref[...]


def tied(block, token):
    if token is None:
        return block
    token = token if isinstance(token, tuple) else (token,)
    return lax.optimization_barrier((block, *token))[0]


def forward_steps(rows, mod, weights):
    w_qkv, b_qkv, w_out, b_out, w_fc1, b_fc1, w_fc2 = weights
    size, width = rows.shape
    local = w_out[0].shape[1]
    hidden = w_fc1[0].shape[1]
    token = yield None, ()
    early, mod = mod
    (normed,) = call(first_norm_kernel, (rows, early), [like(size, width, BF)], token=token)
    normed_far = swap(normed, 2)
    triple_outs = [like(size, 6 * local, BF), like(size, 2 * local, BF), like(size, 2 * local, BF)]
    triple, *sends = call(triple_kernel, (normed, *w_qkv, b_qkv), triple_outs)
    away = [swap(send, 1) for send in sends]
    token = yield triple, ()
    normed_far = tied(normed_far, token)
    triple_far, *sends = call(triple_kernel, (normed_far, *w_qkv, b_qkv), triple_outs, token=token)
    tokens = (triple, triple_far, *away, *(swap(send, 1) for send in sends))
    mixed, log, keep, send = call(
        attend_kernel,
        (*tokens, *w_out),
        [
            like(2 * size, 2 * local, BF),
            like(2 * local // HD, 2 * size, F32),
            like(size, width, F32),
            like(size, width, BF),
        ],
        token=token,
    )
    far = swap(send, 2)
    token = yield keep, ()
    branch, middle, second = call(
        middle_kernel,
        (keep, tied(far, token), b_out[0:1], rows, mod),
        [like(size, width, BF), like(size, width, F32), like(size, width, BF)],
        token=token,
    )
    second_far = swap(second, 2)
    outs = [like(size, 2 * hidden, BF), like(size, 2 * hidden, BF)]
    scratch = [pltpu.VMEM((size, 2 * hidden), BF)]
    act, slope, keep = call(
        mlp_kernel,
        (second, *w_fc1, b_fc1, *w_fc2),
        [*outs, like(size, width, F32)],
        scratch=scratch,
    )
    token = yield keep, ()
    second_far = tied(second_far, token)
    act_far, slope_far, send = call(
        mlp_kernel,
        (second_far, *w_fc1, b_fc1, *w_fc2),
        [*outs, like(size, width, BF)],
        scratch=scratch,
        token=token,
    )
    far = swap(send, 2)
    token = yield send, ()
    feed, result = call(
        layer_end_kernel,
        (keep, tied(far, token), b_out[1:2], middle, mod),
        [like(size, width, BF), like(size, width, BF)],
        token=token,
    )
    state = (
        rows, (normed, normed_far), tokens, mixed, log, branch, middle,
        (second, second_far), (act, act_far), (slope, slope_far), feed,
    )
    return result, state


def backward_steps(grad, mod, weights, state, flops=0):
    w_qkv, b_qkv, w_out, b_out, w_fc1, b_fc1, w_fc2 = weights
    rows, normed, tokens, mixed, log, branch, middle, second, acts, slopes, feed = state
    mod = mod[1]
    size, width = rows.shape
    local = w_out[0].shape[1]
    hidden = w_fc1[0].shape[1]
    token = yield None, ()
    feed_rows, sums_feed = call(
        grad_feed_kernel, (grad, feed, mod), [like(size, width, BF), like(2, width, F32)], token=token
    )
    feed_far = swap(feed_rows, 2)
    outs = [like(size, 2 * hidden, BF), like(1, 2 * hidden, F32)]
    scratch = [
        pltpu.VMEM((size, 2 * hidden), BF),
        pltpu.VMEM((size, 2 * hidden), BF),
        pltpu.SemaphoreType.DMA((2, 2)),
    ]
    hidden_near, sums_near, keep = call(
        grad_mlp_kernel,
        (feed_rows, *w_fc2, slopes[0], *w_fc1),
        [*outs, like(size, width, F32)],
        scratch=scratch,
        far_in=(3,),
        far_out=(0,),
    )
    token = yield keep, ()
    feed_far = tied(feed_far, token)
    hidden_far, sums_far, send = call(
        grad_mlp_kernel,
        (feed_far, *w_fc2, slopes[1], *w_fc1),
        [*outs, like(size, width, BF)],
        scratch=scratch,
        token=token,
        far_in=(3,),
        far_out=(0,),
    )
    far = swap(send, 2)
    token = yield send, ((3, (feed_rows, feed_far), acts),)
    grad_middle, branch_rows, sums_middle = call(
        grad_middle_kernel,
        (keep, tied(far, token), middle, branch, grad, mod),
        [like(size, width, F32), like(size, width, BF), like(4, width, F32)],
        token=token,
    )
    branch_far = swap(branch_rows, 2)
    token = yield branch_rows, ((2, second, (hidden_near, hidden_far)),)
    branch_far = tied(branch_far, token)
    queries, kept, send = call(
        grad_attend_kernel,
        (branch_rows, branch_far, *w_out, *tokens, mixed, log),
        [
            like(2 * size, 2 * local, BF),
            like(2 * size, 4 * local, F32),
            like(2 * size, 4 * local, BF),
        ],
        scratch=[pltpu.VMEM((2 * size, 2 * local), BF)],
        token=token,
        flops=flops,
    )
    got = swap(send, 1)
    token = yield kept, ((1, (branch_rows, branch_far), (mixed,)),)
    outs = [like(size, 6 * local, BF), like(size, width, BF), like(1, 6 * local, F32)]
    triple_far, send, sums_triple_far = call(
        functools.partial(grad_normed_kernel, 1), (queries, kept, got, *w_qkv), outs, token=token
    )
    far = swap(send, 2)
    outs[1] = like(size, width, F32)
    triple_near, keep, sums_triple = call(
        functools.partial(grad_normed_kernel, 0), (queries, kept, got, *w_qkv), outs, token=send
    )
    token = yield keep, ((0, normed, (triple_near, triple_far)),)
    grad_rows, sums_rows = call(
        grad_rows_kernel,
        (keep, tied(far, token), rows, grad_middle, mod),
        [like(size, width, BF), like(2, width, F32)],
        token=token,
    )
    return grad_rows, (sums_rows, sums_middle, sums_feed, sums_triple, sums_triple_far, sums_near, sums_far)


def small_sums(raw):
    sums_rows, sums_middle, sums_feed, sums_triple, sums_triple_far, sums_near, sums_far = raw
    grad_mod = jnp.concatenate(
        [sums_rows, sums_middle[2:3], sums_middle[0:2], sums_feed[0:1]], 0
    ).reshape(1, -1)
    return grad_mod, (
        (sums_triple + sums_triple_far)[0],
        (sums_near + sums_far)[0],
        jnp.concatenate([sums_middle[3:4], sums_feed[1:2]], 0),
    )


def chain_steps(ends, mod, weights, flops):
    sent, state_one = yield from forward_steps(ends, mod, weights)
    arrived = lax.ppermute(sent, "section", [(0, 1)])
    yield sent, ()
    out, state_two = yield from forward_steps(arrived, mod, weights)
    yield out, ()
    back_two = yield from backward_steps(ends, mod, weights, state_two)
    arrived = lax.ppermute(back_two[0], "section", [(1, 0)])
    yield back_two[0], ()
    back_one = yield from backward_steps(arrived, mod, weights, state_one, flops)
    yield back_one[0], ()
    return out, back_two, back_one


def side_by_side(chains, section):
    results = [None] * len(chains)
    products, sums, pending, begun = {}, {}, [], [None, None]
    after = {0: 2}
    for chain in chains:
        next(chain)
    token = None
    while pending or any(result is None for result in results):
        ready = {}
        if any(which == 0 for which, _, _ in pending):
            token = (token, sums[3])
        for i, chain in enumerate(chains):
            try:
                token, made = chain.send(token)
            except StopIteration as stop:
                results[i] = stop.value
                continue
            for which, lefts, rights in made:
                both = ready.setdefault(which, ([], []))
                both[0].extend(lefts)
                both[1].extend(rights)
        for which, keep, got in pending:
            parts = (keep, *got)
            if which == 1:
                waiting = parts
                continue
            if which in after:
                token = (token, sums[after[which]])
                parts = (*parts, *waiting)
            rows, cols = keep.shape[0], sum(x.shape[1] for x in parts[:: 1 + CHUNKS])
            count = len(parts) // (1 + CHUNKS)
            (token,) = call(
                functools.partial(add_kernel, count),
                parts,
                [like(rows, cols, BF)],
                scratch=[
                    pltpu.VMEM((rows, cols), BF),
                    pltpu.VMEM((rows, cols), BF),
                    pltpu.SemaphoreType.DMA((2 * CHUNKS * count,)),
                ],
                token=token,
                far_in=range(len(parts)),
            )
            if which in after and lax.axis_size("dp") <= 4:
                sums[which], begun = line_reduce(token)
            else:
                sums[which] = lax.psum_scatter(token, "dp", scatter_dimension=0, tiled=True)
        pending = []
        for which, operands in ready.items():
            if which not in products:
                products[which] = operands
                continue
            keep, *sends = weight_grad(operands, products[which], section, token)
            token = keep
            pending.append((which, keep, [swap(send, 1) for send in sends]))
    return results, sums, token, begun


def body(
    boundary,
    conditioning,
    query_key_value_weight,
    query_value_bias,
    attention_output_weight,
    output_biases,
    first_mlp_weight,
    first_mlp_bias,
    second_mlp_weight,
    w_ada,
    ada_bias,
):
    leading = lax.axis_index("section") == 0
    ends = boundary[0]
    width, _, local = query_key_value_weight.shape[1:]
    tensor_no = lax.axis_index("tensor")
    dp_no = lax.axis_index("dp")
    tensor_count = lax.axis_size("tensor")
    dp_count = lax.axis_size("dp")
    w_qkv = jnp.concatenate([query_key_value_weight[0, :, i] for i in range(3)], 1)
    qv = query_value_bias[0].astype(F32)
    b_qkv = jnp.concatenate([qv[0], jnp.zeros_like(qv[0]), qv[1]])[None]
    w_out, w_fc1, w_fc2 = attention_output_weight[0], first_mlp_weight[0], second_mlp_weight[0]
    hidden = w_fc1.shape[1]
    vectors = jnp.concatenate([b_qkv, first_mlp_bias.astype(F32)], 1)
    other = swap(vectors, 1)
    weights = (
        (w_qkv, swap(w_qkv, 1)),
        jnp.concatenate([b_qkv, other[:, : 3 * local]], 1),
        (w_out, swap(w_out, 1)),
        output_biases[0].astype(F32),
        (w_fc1, swap(w_fc1, 1)),
        jnp.concatenate([vectors[:, 3 * local :], other[:, 3 * local :]], 1),
        (w_fc2, swap(w_fc2, 1)),
    )
    ada_weight = w_ada[0]
    cond_vals = conditioning.astype(F32)
    cond_act = jax.nn.silu(cond_vals).astype(BF)
    shift = ada_bias[0].astype(F32)
    mods = [
        (dot_nn(cond_act, ada_weight[:, part]) + shift[part]).reshape(2, -1, width)
        for part in (slice(0, 2 * width), slice(2 * width, 6 * width))
    ]
    mods = [(mods[0][b], jnp.concatenate([mods[0][b], mods[1][b]], 0)) for b in range(2)]

    section = lax.axis_index("section").astype(jnp.int32).reshape(1)
    chains, sums, token, begun = side_by_side(
        [chain_steps(ends[b], mods[b], weights, b * 10**11) for b in range(ends.shape[0])], section
    )
    outs = [chain[0] for chain in chains]
    raw = [(chain[1][1], chain[2][1]) for chain in chains]
    leaves, kind = jax.tree.flatten(raw)
    raw = jax.tree.unflatten(kind, lax.optimization_barrier((*leaves, token))[:-1])
    backs_two = [(chain[1][0], *small_sums(two)) for chain, (two, _) in zip(chains, raw)]
    backs_one = [(chain[2][0], *small_sums(one)) for chain, (_, one) in zip(chains, raw)]

    g_both, g_fc1, g_fc2 = (sums[i].astype(F32) for i in (0, 2, 3))
    g_qkv, g_proj = g_both[:, : 3 * local], g_both[:, 3 * local :]
    g_qkv = jnp.stack([g_qkv[:, i * local : (i + 1) * local] for i in range(3)], 1)

    pick = lambda one, two: jnp.where(leading, one, two)
    grad_mods = jnp.concatenate(
        [pick(one[1], two[1]) for one, two in zip(backs_one, backs_two)], 0
    )
    owned_triple, owned_hidden, partial = (
        pick(
            backs_one[0][2][i] + backs_one[1][2][i],
            backs_two[0][2][i] + backs_two[1][2][i],
        )
        for i in range(3)
    )
    def placed(vector):
        size = vector.shape[0] // 2
        full = jnp.zeros((tensor_count * size,), F32)
        for part, where in ((vector[:size], tensor_no), (vector[size:], tensor_no ^ 1)):
            full = lax.dynamic_update_slice(full, part, (where * size,))
        return full

    span = 3 * local
    queries = jnp.concatenate([owned_triple[:local], owned_triple[span : span + local]])
    values = jnp.concatenate([owned_triple[2 * local : span], owned_triple[span + 2 * local :]])
    flat = jnp.concatenate(
        [
            grad_mods.reshape(-1),
            placed(queries),
            placed(values),
            placed(owned_hidden),
            partial.reshape(-1),
        ]
    )
    (flat,) = call(
        copy_kernel, (flat.reshape(-1, width),), [like(flat.size // width, width, F32)], token=token, flops=10**11
    )
    flat = tensor_sum(flat).reshape(-1)
    grad_mods = flat[: 12 * width].reshape(2, 6 * width)
    biases = flat[12 * width :]
    rest, terms = grad_mods, []
    for _ in range(3):
        terms.append(lax.reduce_precision(rest, 8, 7))
        rest = rest - terms[-1]
    back_cond = dot_nt(jnp.concatenate(terms, 0).astype(BF), ada_weight)
    back_cond = tied(back_cond.reshape(3, 2, width).sum(0), begun[0])
    cond_total = back_cond + lax.ppermute(back_cond, "section", [(0, 1), (1, 0)])
    begun = [begun[0], (cond_total, *(begun[1] or ()))]
    everything = over_dp(
        jnp.concatenate([grad_mods.reshape(-1), biases, cond_act.astype(F32).reshape(-1)])[None], begun[:2]
    )
    mods_end = 12 * width
    all_mods = everything[:, :mods_end].reshape(2 * dp_count, 6 * width)
    all_acts = everything[:, -2 * width :].reshape(2 * dp_count, width)
    biases = jnp.sum(everything[:, mods_end : -2 * width], axis=0)
    place = dp_no * tensor_count + tensor_no
    shares = dp_count * tensor_count

    def own_share(vector):
        size = vector.shape[0] // shares
        return lax.dynamic_slice(vector, (place * size,), (size,))[None]

    hidden_all = biases.shape[0] - 4 * width
    g_qv_bias = own_share(biases[: 2 * width])
    g_fc1_bias = own_share(biases[2 * width : 2 * width + hidden_all])
    g_out_bias = own_share(biases[2 * width + hidden_all :])
    g_ada_bias = own_share(jnp.sum(all_mods, axis=0))
    share = width // shares
    act_share = lax.dynamic_slice(all_acts, (0, place * share), (all_acts.shape[0], share))
    g_ada = lax.dot_general(
        act_share, all_mods, (((0,), (0,)), ((), ())), precision=precise, preferred_element_type=F32
    )

    sig = jax.nn.sigmoid(cond_vals)
    cond_grad = cond_total * sig * (1.0 + cond_vals * (1.0 - sig))

    rows_out = jnp.stack([pick(back[0], out) for back, out in zip(backs_one, outs)])[None]
    return (
        rows_out,
        cond_grad,
        g_qkv[None],
        g_qv_bias,
        g_proj[None],
        g_out_bias,
        g_fc1[None],
        g_fc1_bias,
        g_fc2[None],
        g_ada[None],
        g_ada_bias,
    )


def solution(mesh):
    in_specs = (
        P("section", "dp", "tensor", None),
        P("dp", None),
        P("section", None, None, "tensor"),
        P("section", None, "tensor"),
        P("section", None, "tensor"),
        P("section", None, None),
        P("section", None, "tensor"),
        P("section", "tensor"),
        P("section", None, "tensor"),
        P("section", None, None),
        P("section", None),
    )
    out_specs = (
        P("section", "dp", "tensor", None),
        P("dp", None),
        P("section", "dp", None, "tensor"),
        P("section", ("dp", "tensor")),
        P("section", "dp", "tensor"),
        P("section", ("dp", "tensor")),
        P("section", "dp", "tensor"),
        P("section", ("dp", "tensor")),
        P("section", "dp", "tensor"),
        P("section", ("dp", "tensor"), None),
        P("section", ("dp", "tensor")),
    )
    return jax.shard_map(body, mesh=mesh, in_specs=in_specs, out_specs=out_specs, check_vma=False)
```
